32 devices in a mesh: blk: 8 (over y, x, core), uly: 4 (over z).
Axes of the slice: x: 2, y: 2, z: 4, core: 2. Of those that a mesh axis runs over, the one named last changes fastest.
Arguments:
- queries: bfloat16 [8192, 4096], P(('blk', 'uly')), may hold values from -6 to 6
- keys: bfloat16 [8192, 4096], P(('blk', 'uly')), may hold values from -6 to 6
- values: bfloat16 [8192, 4096], P(('blk', 'uly')), may hold values from -6 to 6
- doc_start: int32 [8192], P('blk'), may hold values from 0 to 8191, as said below
Outputs:
- attended: bfloat16 [8192, 4096], P(('blk', 'uly'))
The draws below stay inside these ranges and needn't reach their ends.
Inputs may be any that keep to these rules, and one draw needn't show every extreme that they name: doc_start[0] = 0, and for t > 0 doc_start[t] is either t or doc_start[t - 1].
All inputs are finite; a program needn't handle non-finite values.
Results may differ from the reference program's by a relative error of at most 0.0026.
Values may be sent and summed in bfloat16 or wider, within the bound.
No kernel may reach another device: no remote copies, remote signals or barrier semaphores. Data moves between devices by JAX's collectives and lax.ppermute only.
A program may use at most 128 MiB of HBM per device.

```python
import math
import jax
import jax.numpy as jnp
from jax import lax

HEADS = 32
HEAD_DIM = 128
TOKENS = 8192
WINDOW = 512
QBLOCK = 512


def doc_starts(key):
    base_key = jax.random.fold_in(key, 7)
    region_len = WINDOW // 2
    position = jnp.arange(TOKENS, dtype=jnp.int32)
    region = position // region_len
    top_power = int(math.log2(2 * WINDOW))
    powers = jax.random.randint(jax.random.fold_in(base_key, 1), (TOKENS // region_len + 1,), 3, top_power + 1)
    spans = (2 ** powers).astype(jnp.int32)
    rolls = jax.random.randint(jax.random.fold_in(base_key, 2), (TOKENS,), 0, spans[region])
    marked = (rolls == 0) | (position == 0) | (position == TOKENS - 1)
    return lax.cummax(jnp.where(marked, position, 0), axis=0)


def base_field(key):
    width = HEADS * HEAD_DIM
    return jnp.clip(jax.random.normal(key, (TOKENS, width), jnp.float32), -6.0, 6.0)


def draw_doc_start(key, part):
    return doc_starts(key)


def draw_queries(key, part):
    field = base_field(jax.random.fold_in(key, 11))
    return field.astype(jnp.bfloat16)


def draw_keys(key, part):
    field = base_field(jax.random.fold_in(key, 12))
    return field.astype(jnp.bfloat16)


def level_of(key, extent, shards, smallest, high):
    factor_of = 1.0
    for axis_at, blocks in shards:
        heights = jax.random.uniform(jax.random.fold_in(jax.random.fold_in(key, 6), axis_at), (blocks,), jnp.float32, smallest / len(shards), high / len(shards))
        factor_of = factor_of * jnp.repeat(jnp.exp(heights), extent[axis_at] // blocks).reshape((-1,) + (1,) * (len(extent) - 1 - axis_at))
    return factor_of


def noise(key, extent, deviation, bound, split=(), kind=jnp.bfloat16):
    values = deviation * jax.random.normal(key, extent, jnp.float32)
    if split:
        values = values * level_of(key, extent, split, -0.22, 0.18)
    return jnp.clip(values, -bound, bound).astype(kind)


def setup_inputs(seed: int = 0) -> dict:
    arg_keys = jax.random.split(jax.random.key(seed), 5)
    queries = draw_queries(jax.random.fold_in(arg_keys[4], 71), 0)
    keys = draw_keys(jax.random.fold_in(arg_keys[4], 71), 0)
    values = noise(arg_keys[2], (TOKENS, HEADS * HEAD_DIM), 1.0, 6.0, ((0, 32),))
    doc_start = draw_doc_start(jax.random.fold_in(arg_keys[4], 71), 0)
    return dict(queries=queries, keys=keys, values=values, doc_start=doc_start)


def reference(queries, keys, values, doc_start):
    total = queries.shape[0]
    width = HEADS * HEAD_DIM
    query_all = queries.reshape(total, HEADS, HEAD_DIM)
    padding = jnp.zeros((WINDOW, width), keys.dtype)
    keys_wide = jnp.concatenate([padding, keys], axis=0).reshape(total + WINDOW, HEADS, HEAD_DIM)
    values_wide = jnp.concatenate([padding, values], axis=0).reshape(total + WINDOW, HEADS, HEAD_DIM)
    score_scale = 1.0 / math.sqrt(HEAD_DIM)

    def attend_block(block_index):
        first = (block_index * QBLOCK).astype(jnp.int32)
        query_rows = lax.dynamic_slice_in_dim(query_all, first, QBLOCK, 0).astype(jnp.float32)
        key_rows = lax.dynamic_slice_in_dim(keys_wide, first, QBLOCK + WINDOW, 0).astype(jnp.float32)
        value_rows = lax.dynamic_slice_in_dim(values_wide, first, QBLOCK + WINDOW, 0).astype(jnp.float32)
        starts = lax.dynamic_slice_in_dim(doc_start, first, QBLOCK, 0)
        query_pos = first + jnp.arange(QBLOCK, dtype=jnp.int32)
        key_pos = first - WINDOW + jnp.arange(QBLOCK + WINDOW, dtype=jnp.int32)
        allowed = (key_pos[None, :] <= query_pos[:, None]) & (key_pos[None, :] > query_pos[:, None] - WINDOW) & (key_pos[None, :] >= starts[:, None])
        scores = jnp.einsum('qhd,khd->hqk', query_rows, key_rows) * score_scale
        scores = jnp.where(allowed[None], scores, -jnp.inf)
        row_max = lax.optimization_barrier(jnp.max(scores, axis=-1, keepdims=True))
        probs = jnp.exp(scores - row_max)
        totals = lax.optimization_barrier(jnp.sum(probs, axis=-1))
        weights = probs.astype(jnp.bfloat16)
        mixed = jnp.einsum('hqk,khd->qhd', weights.astype(jnp.float32), value_rows)
        mixed = mixed / jnp.transpose(totals)[:, :, None]
        return mixed.astype(jnp.bfloat16).reshape(QBLOCK, width)
    blocks = lax.map(attend_block, jnp.arange(total // QBLOCK, dtype=jnp.int32))
    return blocks.reshape(total, width)
```

```python
import functools
import math

import jax
import jax.numpy as jnp
from jax import lax
from jax.experimental import pallas as pl
from jax.experimental.pallas import tpu as pltpu
from jax.sharding import PartitionSpec as P

HEADS = 32
HEAD_DIM = 128
WINDOW = 512
TILE = 128
ROWS = 32
PIECES = 4
BELOW = -1e30


def split_heads(sources, groups, group_heads, piece, piece_heads):
    tokens = sources[0].shape[0]
    wide = piece_heads * HEAD_DIM

    def kernel(*refs):
        ins, out, sems = refs[: len(sources)], refs[len(sources)], refs[len(sources) + 1]
        copies = []
        for at, src in enumerate(ins):
            for g in range(groups):
                first = (g * group_heads + piece * piece_heads) * HEAD_DIM
                copies.append(
                    pltpu.make_async_copy(
                        src.at[:, pl.ds(first, wide)],
                        out.at[g, :, pl.ds(at * wide, wide)],
                        sems.at[at * groups + g],
                    )
                )
        for copy in copies:
            copy.start()
        for copy in copies:
            copy.wait()

    return pl.pallas_call(
        kernel,
        out_shape=jax.ShapeDtypeStruct((groups, tokens, len(sources) * wide), sources[0].dtype),
        in_specs=[pl.BlockSpec(memory_space=pl.ANY)] * len(sources),
        out_specs=pl.BlockSpec(memory_space=pl.ANY),
        scratch_shapes=[pltpu.SemaphoreType.DMA((len(sources) * groups,))],
        cost_estimate=pl.CostEstimate(
            flops=0, bytes_accessed=4 * groups * tokens * len(sources) * wide, transcendentals=0
        ),
        name="split_heads",
    )(*sources)


def join_heads(pieces, group_heads, piece_heads):
    groups, tokens, wide = pieces[0].shape

    def kernel(*refs):
        ins, out, sems = refs[: len(pieces)], refs[len(pieces)], refs[len(pieces) + 1]
        copies = []
        for at, src in enumerate(ins):
            for g in range(groups):
                first = (g * group_heads + at * piece_heads) * HEAD_DIM
                copies.append(
                    pltpu.make_async_copy(
                        src.at[g], out.at[:, pl.ds(first, wide)], sems.at[at * groups + g]
                    )
                )
        for copy in copies:
            copy.start()
        for copy in copies:
            copy.wait()

    return pl.pallas_call(
        kernel,
        out_shape=jax.ShapeDtypeStruct((tokens, groups * group_heads * HEAD_DIM), pieces[0].dtype),
        in_specs=[pl.BlockSpec(memory_space=pl.ANY)] * len(pieces),
        out_specs=pl.BlockSpec(memory_space=pl.ANY),
        scratch_shapes=[pltpu.SemaphoreType.DMA((len(pieces) * groups,))],
        cost_estimate=pl.CostEstimate(
            flops=0, bytes_accessed=4 * len(pieces) * groups * tokens * wide, transcendentals=0
        ),
        name="join_heads",
    )(*pieces)


def pack(blocks, plan, slots):
    _, rows, wide = blocks.shape
    stretches = plan.shape[1]

    def kernel(plan_ref, in_ref, out_ref):
        for b in range(stretches):
            src, dst, count = plan_ref[0, b], plan_ref[1, b], plan_ref[2, b]

            def move(j, carry, src=src, dst=dst):
                out_ref[dst + j] = in_ref[src + j]
                return carry

            lax.fori_loop(0, count, move, 0)

    return pl.pallas_call(
        kernel,
        out_shape=jax.ShapeDtypeStruct((slots, rows, wide), blocks.dtype),
        in_specs=[pl.BlockSpec(memory_space=pltpu.SMEM), pl.BlockSpec(memory_space=pltpu.VMEM)],
        out_specs=pl.BlockSpec(memory_space=pltpu.VMEM),
        compiler_params=pltpu.CompilerParams(vmem_limit_bytes=32 * 1024 * 1024),
        cost_estimate=pl.CostEstimate(
            flops=0, bytes_accessed=2 * (blocks.size + slots * rows * wide), transcendentals=0
        ),
        name="pack_halo",
    )(plan, blocks)


def attention(plan, lows, query, local, near, far, heads):
    stretches, tokens, wide = query.shape
    tiles = tokens // TILE
    most = WINDOW // TILE + 1
    halo = WINDOW // ROWS
    chunk = tokens // ROWS
    scale = math.log2(math.e) / math.sqrt(HEAD_DIM)

    def kernel(plan_ref, lows_ref, q_ref, local_ref, near_ref, far_ref, out_ref, held):
        b = pl.program_id(0)

        @pl.when(b == 0)
        def _():
            held[...] = jnp.zeros_like(held)

        held[halo:] = local_ref[0].reshape(chunk, ROWS, 2 * wide)
        for ref, at, end in ((near_ref, 0, halo), (far_ref, 2, halo - chunk)):
            first, count = plan_ref[at, b], plan_ref[at + 1, b]

            def move(j, carry, ref=ref, first=first, to=end - count):
                held[to + j] = ref[first + j]
                return carry

            lax.fori_loop(0, count, move, 0)

        for i in range(tiles):
            need = plan_ref[4 + i, b]
            low = jnp.broadcast_to(lows_ref[0, :, i * TILE : (i + 1) * TILE], (TILE, TILE)).T
            for m in range(1, most + 1):

                @pl.when(need == m)
                def _(i=i, m=m, low=low):
                    first = WINDOW + (i + 1 - m) * TILE
                    at = lax.broadcasted_iota(jnp.int32, (TILE, TILE), 1)
                    row = lax.broadcasted_iota(jnp.int32, (TILE, TILE), 0)
                    bias = []
                    for j in range(m):
                        allowed = (at + (first + j * TILE)).astype(jnp.float32) >= low
                        if j == m - 1:
                            allowed = allowed & (at <= row)
                        bias.append(jnp.where(allowed, 0.0, BELOW))
                    bias = jnp.concatenate(bias, axis=1)
                    span = pl.ds(first // ROWS, m * TILE // ROWS)
                    for h in range(heads):
                        q = q_ref[0, i * TILE : (i + 1) * TILE, h * HEAD_DIM : (h + 1) * HEAD_DIM]
                        k = held[span, :, h * HEAD_DIM : (h + 1) * HEAD_DIM].reshape(m * TILE, HEAD_DIM)
                        v = held[span, :, wide + h * HEAD_DIM : wide + (h + 1) * HEAD_DIM].reshape(
                            m * TILE, HEAD_DIM
                        )
                        scores = bias + lax.dot_general(
                            q, k, (((1,), (1,)), ((), ())), preferred_element_type=jnp.float32
                        )
                        row_max = jnp.max(scores, axis=1, keepdims=True)
                        probs = jnp.exp2((scores - row_max) * scale)
                        totals = jnp.sum(probs, axis=1, keepdims=True)
                        mixed = jnp.dot(probs.astype(jnp.bfloat16), v, preferred_element_type=jnp.float32)
                        out_ref[0, i * TILE : (i + 1) * TILE, h * HEAD_DIM : (h + 1) * HEAD_DIM] = (
                            mixed / totals
                        ).astype(jnp.bfloat16)

    whole = lambda array: pl.BlockSpec(array.shape, lambda b: (0,) * array.ndim)
    return pl.pallas_call(
        kernel,
        grid=(stretches,),
        out_shape=jax.ShapeDtypeStruct(query.shape, query.dtype),
        in_specs=[
            pl.BlockSpec(memory_space=pltpu.SMEM),
            pl.BlockSpec((1, 1, tokens), lambda b: (b, 0, 0)),
            pl.BlockSpec((1, tokens, wide), lambda b: (b, 0, 0)),
            pl.BlockSpec((1, tokens, 2 * wide), lambda b: (b, 0, 0)),
            whole(near),
            whole(far),
        ],
        out_specs=pl.BlockSpec((1, tokens, wide), lambda b: (b, 0, 0)),
        scratch_shapes=[pltpu.VMEM((halo + chunk, ROWS, 2 * wide), jnp.bfloat16)],
        compiler_params=pltpu.CompilerParams(
            dimension_semantics=("arbitrary",), vmem_limit_bytes=48 * 1024 * 1024
        ),
        cost_estimate=pl.CostEstimate(
            flops=4 * stretches * tokens * heads * HEAD_DIM * 3 * TILE,
            bytes_accessed=2 * (2 * query.size + local.size + near.size + far.size),
            transcendentals=stretches * tokens * heads * 3 * TILE,
        ),
        name="attention",
    )(plan, lows, query, local, near, far)


def shards(groups, ring, queries, keys, values, doc_start):
    tokens = queries.shape[0]
    group_heads = HEADS // groups
    pieces = min(PIECES, group_heads)
    piece_heads = group_heads // pieces
    chunk = tokens // ROWS
    plane = lax.axis_index("uly")

    starts = lax.all_gather(doc_start, "blk", axis=0, tiled=True)
    chunks = groups * ring
    by_chunk = starts.reshape(chunks, tokens)
    opens = jnp.arange(chunks, dtype=jnp.int32) * tokens
    need = jnp.minimum(opens - by_chunk[:, 0], WINDOW - 1)
    near_need = (jnp.minimum(need, tokens) + ROWS - 1) // ROWS
    far_need = (jnp.maximum(need - tokens, 0) + ROWS - 1) // ROWS
    near_sum = jnp.max(jnp.sum(near_need.reshape(groups, ring), axis=0))
    far_sum = jnp.max(jnp.sum(far_need.reshape(groups, ring), axis=0))

    def mine(per_chunk, ahead):
        padded = jnp.concatenate([per_chunk, jnp.zeros((ring,), jnp.int32)])
        rolled = lax.dynamic_slice_in_dim(padded, plane + ahead, chunks, 0)
        return rolled.reshape(groups, ring)[:, 0]

    def before(counts):
        earlier = jnp.arange(groups)[None, :] < jnp.arange(groups)[:, None]
        return jnp.sum(jnp.where(earlier, counts[None, :], 0), axis=1)

    near_in, far_in = mine(near_need, 0), mine(far_need, 0)
    near_out, far_out = mine(near_need, 1), mine(far_need, 1)
    near_first, far_first = before(near_in), before(far_in)
    own_first = jnp.arange(groups, dtype=jnp.int32) * chunk + chunk - near_out
    near_plan = jnp.stack([own_first, before(near_out), near_out])
    far_plan = jnp.stack([near_first + near_in - far_out, before(far_out), far_out])

    mine_starts = lax.dynamic_index_in_dim(
        starts.reshape(groups, ring, tokens), plane, 1, keepdims=False
    )
    position = (jnp.arange(groups, dtype=jnp.int32)[:, None] * ring + plane) * tokens + jnp.arange(
        tokens, dtype=jnp.int32
    )[None, :]
    window_open = position[:, :1] - WINDOW
    lows = jnp.maximum(mine_starts, position - (WINDOW - 1)) - window_open
    tile_low = lows[:, ::TILE]
    tile_end = WINDOW + TILE * (1 + jnp.arange(tokens // TILE, dtype=jnp.int32))
    tile_need = (tile_end[None, :] - tile_low + TILE - 1) // TILE
    plan = jnp.concatenate(
        [jnp.stack([near_first, near_in, far_first, far_in]), tile_need.T.astype(jnp.int32)]
    )
    lows = lows.astype(jnp.float32)[:, None, :]

    def spread(array):
        return lax.all_to_all(array, "blk", split_axis=0, concat_axis=0, tiled=True)

    def onward(array):
        return lax.ppermute(array, "uly", [(i, (i + 1) % ring) for i in range(ring)])

    def run(near_slots, far_slots, queries, keys, values, near_plan, far_plan, plan, lows):
        done = []
        for piece in range(pieces):
            local = spread(split_heads((keys, values), groups, group_heads, piece, piece_heads))
            blocks = local.reshape(groups * chunk, ROWS, local.shape[2])
            near = onward(pack(blocks, near_plan, near_slots))
            far = onward(pack(near, far_plan, far_slots))
            query = spread(split_heads((queries,), groups, group_heads, piece, piece_heads))
            done.append(spread(attention(plan, lows, query, local, near, far, piece_heads)))
        return join_heads(done, group_heads, piece_heads)

    full = groups * chunk
    return run(full, full, queries, keys, values, near_plan, far_plan, plan, lows)


def solution(mesh):
    return jax.shard_map(
        functools.partial(shards, mesh.shape["blk"], mesh.shape["uly"]),
        mesh=mesh,
        in_specs=(
            P(("blk", "uly"), None),
            P(("blk", "uly"), None),
            P(("blk", "uly"), None),
            P("blk"),
        ),
        out_specs=P(("blk", "uly"), None),
        check_vma=False,
    )
```

```python
import functools
import math

import jax
import jax.numpy as jnp
from jax import lax
from jax.experimental import pallas as pl
from jax.experimental.pallas import tpu as pltpu
from jax.sharding import PartitionSpec as P

HEADS = 32
HEAD_DIM = 128
WINDOW = 512
TILE = 128
ROWS = 32
BELOW = -1e30
UNROLLED = 3
SIZES = {3: (1, 2)}
ROOMS = ((34, 10), (38, 17), (46, 19), (51, 28), (64, 64))


def split_heads(sources, groups, group_heads):
    tokens, columns = sources[0].shape
    wide = group_heads * HEAD_DIM
    rest = columns - groups * wide
    rows = min(2 * ROWS, tokens)

    def kernel(*refs):
        ins, out, other = refs[: len(sources)], refs[-2], refs[-1]
        for at, src in enumerate(ins):
            for g in range(groups):
                out[g, :, at * wide : (at + 1) * wide] = src[:, g * wide : (g + 1) * wide]
            other[0, :, at * rest : (at + 1) * rest] = src[:, groups * wide :]

    widths = (len(sources) * wide, len(sources) * rest)
    return pl.pallas_call(
        kernel,
        grid=(tokens // rows,),
        out_shape=[
            jax.ShapeDtypeStruct((groups, tokens, widths[0]), sources[0].dtype),
            jax.ShapeDtypeStruct((1, tokens, widths[1]), sources[0].dtype),
        ],
        in_specs=[pl.BlockSpec((rows, columns), lambda t: (t, 0))] * len(sources),
        out_specs=[
            pl.BlockSpec((groups, rows, widths[0]), lambda t: (0, t, 0)),
            pl.BlockSpec((1, rows, widths[1]), lambda t: (0, t, 0)),
        ],
        cost_estimate=pl.CostEstimate(
            flops=0, bytes_accessed=4 * len(sources) * sources[0].size, transcendentals=0
        ),
        name="split_heads",
    )(*sources)


def join_heads(pieces, rest):
    groups, tokens, _ = pieces[0].shape
    band = sum(piece.shape[2] for piece in pieces)
    rows = min(2 * ROWS, tokens)

    def kernel(*refs):
        ins, other, out = refs[:-2], refs[-2], refs[-1]
        for g in range(groups):
            first = g * band
            for src in ins:
                out[:, first : first + src.shape[2]] = src[g]
                first += src.shape[2]
        out[:, groups * band :] = other[0]

    columns = groups * band + rest.shape[2]
    return pl.pallas_call(
        kernel,
        grid=(tokens // rows,),
        out_shape=jax.ShapeDtypeStruct((tokens, columns), rest.dtype),
        in_specs=[
            pl.BlockSpec((piece.shape[0], rows, piece.shape[2]), lambda t: (0, t, 0))
            for piece in (*pieces, rest)
        ],
        out_specs=pl.BlockSpec((rows, columns), lambda t: (t, 0)),
        cost_estimate=pl.CostEstimate(flops=0, bytes_accessed=4 * tokens * columns, transcendentals=0),
        name="join_heads",
    )(*pieces, rest)


def pack(blocks, plan, slots, bands):
    _, rows, _ = blocks.shape
    stretches = plan.shape[1]
    wide = sum(end - first for first, end in bands)

    def kernel(plan_ref, in_ref, out_ref):
        def stretch(b, carry):
            src, dst, count = plan_ref[0, b], plan_ref[1, b], plan_ref[2, b]

            def move(j, carry):
                to = 0
                for first, end in bands:
                    out_ref[dst + j, :, to : to + end - first] = in_ref[src + j, :, first:end]
                    to += end - first
                return carry

            return lax.fori_loop(0, count, move, carry)

        lax.fori_loop(0, stretches, stretch, 0)

    return pl.pallas_call(
        kernel,
        out_shape=jax.ShapeDtypeStruct((slots, rows, wide), blocks.dtype),
        in_specs=[pl.BlockSpec(memory_space=pltpu.SMEM), pl.BlockSpec(memory_space=pltpu.VMEM)],
        out_specs=pl.BlockSpec(memory_space=pltpu.VMEM),
        compiler_params=pltpu.CompilerParams(vmem_limit_bytes=32 * 1024 * 1024),
        cost_estimate=pl.CostEstimate(
            flops=0, bytes_accessed=4 * slots * rows * wide, transcendentals=0
        ),
        name="pack_halo",
    )(plan, blocks)


def attention(plan, lows, query, query_heads, local, local_bands, near, far):
    start, heads = query_heads
    stretches, tokens, _ = query.shape
    wide = heads * HEAD_DIM
    tiles = tokens // TILE
    most = WINDOW // TILE + 1
    halo = WINDOW // ROWS
    chunk = tokens // ROWS
    scale = math.log2(math.e) / math.sqrt(HEAD_DIM)

    def attend(m, b, lows_ref, q_ref, out_ref, held):
        at = lax.broadcasted_iota(jnp.int32, (TILE, TILE), 1)
        row = lax.broadcasted_iota(jnp.int32, (TILE, TILE), 0)
        spans, biases = [], []
        for i in range(tiles):
            first = WINDOW + (i + 1 - m) * TILE
            low = lows_ref[b, i * TILE : (i + 1) * TILE]
            bias = []
            for j in range(m):
                allowed = (at + (first + j * TILE)).astype(jnp.float32) >= low
                if j == m - 1:
                    allowed = allowed & (at <= row)
                bias.append(jnp.where(allowed, 0.0, BELOW))
            biases.append(jnp.concatenate(bias, axis=1))
            spans.append(pl.ds(first // ROWS, m * TILE // ROWS))

        def head(h, carry):
            at = lambda base: pl.ds(pl.multiple_of((base + h) * HEAD_DIM, HEAD_DIM), HEAD_DIM)
            for i in range(tiles):
                q = q_ref[b, i * TILE : (i + 1) * TILE, at(start)]
                k = held[spans[i], :, at(0)].reshape(m * TILE, HEAD_DIM)
                v = held[spans[i], :, at(heads)].reshape(m * TILE, HEAD_DIM)
                scores = biases[i] + lax.dot_general(
                    q, k, (((1,), (1,)), ((), ())), preferred_element_type=jnp.float32
                )
                row_max = jnp.max(scores, axis=1, keepdims=True)
                probs = jnp.exp2((scores - row_max) * scale)
                totals = jnp.sum(probs, axis=1, keepdims=True)
                mixed = jnp.dot(probs.astype(jnp.bfloat16), v, preferred_element_type=jnp.float32)
                out_ref[b, i * TILE : (i + 1) * TILE, at(0)] = (mixed / totals).astype(jnp.bfloat16)
            return carry

        if heads <= UNROLLED:
            for h in range(heads):
                head(h, 0)
        else:
            lax.fori_loop(0, heads, head, 0)

    def kernel(plan_ref, lows_ref, q_ref, local_ref, near_ref, far_ref, out_ref, held):
        held[...] = jnp.zeros_like(held)

        def stretch(b, carry):
            for at, (first, end) in enumerate(local_bands):
                held[halo:, :, at * wide : (at + 1) * wide] = local_ref[b, :, first:end].reshape(
                    chunk, ROWS, wide
                )
            for ref, at, end in ((near_ref, 0, halo), (far_ref, 2, halo - chunk)):
                first, count = plan_ref[at, b], plan_ref[at + 1, b]

                def move(j, carry, ref=ref, first=first, to=end - count):
                    held[to + j] = ref[first + j]
                    return carry

                lax.fori_loop(0, count, move, 0)

            need = plan_ref[4, b]
            for m in range(1, most + 1):
                pl.when(need == m)(functools.partial(attend, m, b, lows_ref, q_ref, out_ref, held))
            return carry

        lax.fori_loop(0, stretches, stretch, 0)

    return pl.pallas_call(
        kernel,
        out_shape=jax.ShapeDtypeStruct((stretches, tokens, wide), query.dtype),
        in_specs=[pl.BlockSpec(memory_space=pltpu.SMEM)] + [pl.BlockSpec(memory_space=pltpu.VMEM)] * 5,
        out_specs=pl.BlockSpec(memory_space=pltpu.VMEM),
        scratch_shapes=[pltpu.VMEM((halo + chunk, ROWS, 2 * wide), jnp.bfloat16)],
        compiler_params=pltpu.CompilerParams(vmem_limit_bytes=32 * 1024 * 1024),
        cost_estimate=pl.CostEstimate(
            flops=4 * stretches * tokens * heads * HEAD_DIM * 3 * TILE,
            bytes_accessed=2 * (4 * stretches * tokens * wide + near.size + far.size),
            transcendentals=stretches * tokens * heads * 3 * TILE,
        ),
        name="attention",
    )(plan, lows, query, local, near, far)


def shards(groups, ring, queries, keys, values, doc_start):
    tokens = queries.shape[0]
    group_heads = max(1, 3 * HEADS // (4 * groups))
    rest_heads = HEADS - groups * group_heads
    chunk = tokens // ROWS
    chunks = groups * ring
    plane = lax.axis_index("uly")
    me = lax.axis_index("blk") * ring + plane

    def spread(array):
        return lax.all_to_all(array, "blk", split_axis=0, concat_axis=0, tiled=True)

    def onward(array):
        return lax.ppermute(array, "uly", [(i, (i + 1) % ring) for i in range(ring)])

    def next_chunk(array):
        return lax.ppermute(array, ("blk", "uly"), [(i, i + 1) for i in range(chunks - 1)])

    starts = spread(jnp.broadcast_to(doc_start[None, None], (groups, 1, ring * tokens)))
    by_chunk = starts.reshape(chunks, tokens)
    opens = jnp.arange(chunks, dtype=jnp.int32) * tokens
    need = jnp.minimum(opens - by_chunk[:, 0], WINDOW - 1)
    near_need = (jnp.minimum(need, tokens) + ROWS - 1) // ROWS
    far_need = (jnp.maximum(need - tokens, 0) + ROWS - 1) // ROWS
    near_sum = jnp.max(jnp.sum(near_need.reshape(groups, ring), axis=0))
    far_sum = jnp.max(jnp.sum(far_need.reshape(groups, ring), axis=0))

    def mine(per_chunk, ahead):
        padded = jnp.concatenate([per_chunk, jnp.zeros((ring,), jnp.int32)])
        rolled = lax.dynamic_slice_in_dim(padded, plane + ahead, chunks, 0)
        return rolled.reshape(groups, ring)[:, 0]

    def before(counts):
        earlier = jnp.arange(groups)[None, :] < jnp.arange(groups)[:, None]
        return jnp.sum(jnp.where(earlier, counts[None, :], 0), axis=1)

    near_in, far_in = mine(near_need, 0), mine(far_need, 0)
    near_out, far_out = mine(near_need, 1), mine(far_need, 1)
    near_first = before(near_in)
    own_first = jnp.arange(groups, dtype=jnp.int32) * chunk + chunk - near_out
    near_plan = jnp.stack([own_first, before(near_out), near_out])
    far_plan = jnp.stack([near_first + near_in - far_out, before(far_out), far_out])

    position = jnp.arange(chunks * tokens, dtype=jnp.int32).reshape(chunks, tokens)
    lows = jnp.maximum(by_chunk, position - (WINDOW - 1)) - (opens[:, None] - WINDOW)
    tile_end = WINDOW + TILE * (1 + jnp.arange(tokens // TILE, dtype=jnp.int32))
    tile_need = jnp.max((tile_end[None, :] - lows[:, ::TILE] + TILE - 1) // TILE, axis=1)
    lows = lows.astype(jnp.float32)
    plane_lows = lax.dynamic_index_in_dim(lows.reshape(groups, ring, tokens), plane, 1, keepdims=False)
    plane_lows = jnp.broadcast_to(plane_lows[:, :, None], (groups, tokens, TILE))
    plan = jnp.stack([near_first, near_in, before(far_in), far_in, mine(tile_need, 0)])

    def own(per_chunk):
        return lax.dynamic_index_in_dim(per_chunk, me, 0, keepdims=False)

    own_near, own_far = own(near_need), own(far_need)
    own_plan = jnp.stack([chunk - own_near, own_near, chunk - own_far, own_far, own(tile_need)])[:, None]
    own_lows = jnp.broadcast_to(own(lows)[None, :, None], (1, tokens, TILE))

    wide, rest = group_heads * HEAD_DIM, rest_heads * HEAD_DIM
    pair, own_pair = split_heads((keys, values), groups, group_heads)
    own_next = next_chunk(own_pair)
    own_after = next_chunk(own_next)
    pair = spread(pair)
    later, _ = lax.optimization_barrier((queries, starts))
    query, own_query = split_heads((later,), groups, group_heads)

    def run(room, pair, query, near_plan, far_plan, plan, plane_lows, own_query, own_pair, own_next, own_after, own_plan, own_lows):
        near_slots, far_slots = (groups * chunk * share // 64 for share in room)
        blocks = pair.reshape(groups * chunk, ROWS, 2 * wide)
        pieces = []
        start = 0
        for size in SIZES.get(group_heads, (group_heads,)):
            first, end = start * HEAD_DIM, (start + size) * HEAD_DIM
            pieces.append(((start, size), ((first, end), (wide + first, wide + end))))
            start += size
        packed = [pack(blocks, near_plan, near_slots, bands) for _, bands in pieces]
        query = spread(lax.optimization_barrier((query, packed))[0])
        nears = [onward(packed[0])]
        own_out = attention(
            own_plan, own_lows, own_query, (0, rest_heads), own_pair, ((0, rest), (rest, 2 * rest)),
            own_next.reshape(chunk, ROWS, 2 * rest), own_after.reshape(chunk, ROWS, 2 * rest),
        )
        nears[0], own_out = lax.optimization_barrier((nears[0], own_out))
        for array in packed[1:]:
            nears.append(onward(lax.optimization_barrier((array, nears[-1]))[0]))
        done = []
        for i, (heads, bands) in enumerate(pieces):
            near, _ = lax.optimization_barrier((nears[i], done[:-1]))
            far = onward(pack(near, far_plan, far_slots, ((0, near.shape[2]),)))
            done.append(spread(attention(plan, plane_lows, query, heads, pair, bands, near, far)))
        return join_heads(done, own_out)

    shares = [[groups * chunk * share // 64 for share in room] for room in ROOMS]
    level = sum(
        ((near_sum > near) | (far_sum > far)).astype(jnp.int32) for near, far in shares[:-1]
    )
    return lax.switch(
        level, [functools.partial(run, room) for room in ROOMS],
        pair, query, near_plan, far_plan, plan, plane_lows, own_query, own_pair, own_next, own_after, own_plan, own_lows,
    )


def solution(mesh):
    return jax.shard_map(
        functools.partial(shards, mesh.shape["blk"], mesh.shape["uly"]),
        mesh=mesh,
        in_specs=(
            P(("blk", "uly"), None),
            P(("blk", "uly"), None),
            P(("blk", "uly"), None),
            P("blk"),
        ),
        out_specs=P(("blk", "uly"), None),
        check_vma=False,
    )
```

```python
import functools
import math

import jax
import jax.numpy as jnp
from jax import lax
from jax.experimental import pallas as pl
from jax.experimental.pallas import tpu as pltpu
from jax.sharding import PartitionSpec as P

HEADS = 32
HEAD_DIM = 128
WINDOW = 512
TILE = 128
ROWS = 32
BELOW = -1e30
UNROLLED = 3
ROOMS = ((34, 10), (38, 17), (46, 19), (51, 28), (64, 64))


def split_heads(sources, groups, group_heads, wanted):
    tokens, columns = sources[0].shape
    band = group_heads * HEAD_DIM
    rest = columns - groups * band
    rows = min(2 * ROWS, tokens)
    shapes = [
        (groups if parts[0][2] else 1, rows, sum(size * HEAD_DIM or rest for _, _, size in parts))
        for parts in wanted
    ]

    def kernel(*refs):
        for out, parts in zip(refs[len(sources) :], wanted):
            to = 0
            for which, start, size in parts:
                wide = size * HEAD_DIM or rest
                for g in range(groups if size else 1):
                    first = g * band + start * HEAD_DIM if size else groups * band
                    out[g, :, to : to + wide] = refs[which][:, first : first + wide]
                to += wide

    return pl.pallas_call(
        kernel,
        grid=(tokens // rows,),
        out_shape=[
            jax.ShapeDtypeStruct((shape[0], tokens, shape[2]), sources[0].dtype) for shape in shapes
        ],
        in_specs=[pl.BlockSpec((rows, columns), lambda t: (t, 0))] * len(sources),
        out_specs=[pl.BlockSpec(shape, lambda t: (0, t, 0)) for shape in shapes],
        cost_estimate=pl.CostEstimate(
            flops=0, bytes_accessed=4 * len(sources) * sources[0].size, transcendentals=0
        ),
        name="split_heads",
    )(*sources)


def rest_of(keys, values, rest):
    tokens, columns = keys.shape
    rows = min(4 * ROWS, tokens)

    def kernel(k_ref, v_ref, out_ref):
        out_ref[0, :, :rest] = k_ref[...]
        out_ref[0, :, rest:] = v_ref[...]

    return pl.pallas_call(
        kernel,
        grid=(tokens // rows,),
        out_shape=jax.ShapeDtypeStruct((1, tokens, 2 * rest), keys.dtype),
        in_specs=[pl.BlockSpec((rows, rest), lambda t: (t, columns // rest - 1))] * 2,
        out_specs=pl.BlockSpec((1, rows, 2 * rest), lambda t: (0, t, 0)),
        cost_estimate=pl.CostEstimate(flops=0, bytes_accessed=8 * tokens * rest, transcendentals=0),
        name="rest_of",
    )(keys, values)


def join_heads(pieces, rest):
    groups, tokens, _ = pieces[0].shape
    band = sum(piece.shape[2] for piece in pieces)
    rows = min(2 * ROWS, tokens)

    def kernel(*refs):
        ins, other, out = refs[:-2], refs[-2], refs[-1]
        for g in range(groups):
            first = g * band
            for src in ins:
                out[:, first : first + src.shape[2]] = src[g]
                first += src.shape[2]
        out[:, groups * band :] = other[0]

    columns = groups * band + rest.shape[2]
    return pl.pallas_call(
        kernel,
        grid=(tokens // rows,),
        out_shape=jax.ShapeDtypeStruct((tokens, columns), rest.dtype),
        in_specs=[
            pl.BlockSpec((piece.shape[0], rows, piece.shape[2]), lambda t: (0, t, 0))
            for piece in (*pieces, rest)
        ],
        out_specs=pl.BlockSpec((rows, columns), lambda t: (t, 0)),
        cost_estimate=pl.CostEstimate(flops=0, bytes_accessed=4 * tokens * columns, transcendentals=0),
        name="join_heads",
    )(*pieces, rest)


def pack(blocks, plan, slots, wide):
    rows = blocks.shape[1]
    stretches = plan.shape[1]

    def kernel(plan_ref, in_ref, out_ref):
        def stretch(b, carry):
            src, dst, count = plan_ref[0, b], plan_ref[1, b], plan_ref[2, b]

            def move(j, carry):
                out_ref[dst + j] = in_ref[src + j, :, :wide]
                return carry

            return lax.fori_loop(0, count, move, carry)

        lax.fori_loop(0, stretches, stretch, 0)

    return pl.pallas_call(
        kernel,
        out_shape=jax.ShapeDtypeStruct((slots, rows, wide), blocks.dtype),
        in_specs=[pl.BlockSpec(memory_space=pltpu.SMEM), pl.BlockSpec(memory_space=pltpu.VMEM)],
        out_specs=pl.BlockSpec(memory_space=pltpu.VMEM),
        compiler_params=pltpu.CompilerParams(vmem_limit_bytes=32 * 1024 * 1024),
        cost_estimate=pl.CostEstimate(
            flops=0, bytes_accessed=4 * slots * rows * wide, transcendentals=0
        ),
        name="pack_halo",
    )(plan, blocks)


def attention(plan, lows, query, query_heads, local, near, far, earlier=None, out_at=(0, None)):
    start, heads = query_heads
    out_start, out_heads = out_at[0], out_at[1] or heads
    stretches, tokens, _ = query.shape
    wide = heads * HEAD_DIM
    least, most = tokens // TILE, (WINDOW + tokens) // TILE
    spans = (*range(least, most - 1), most)
    halo = WINDOW // ROWS
    chunk = tokens // ROWS
    scale = math.log2(math.e) / math.sqrt(HEAD_DIM)

    def attend(m, b, lows_ref, q_ref, out_ref, held):
        first = WINDOW + tokens - m * TILE
        key = lax.broadcasted_iota(jnp.int32, (TILE, tokens), 0)
        row = lax.broadcasted_iota(jnp.int32, (TILE, tokens), 1)
        low = jnp.broadcast_to(lows_ref[b], (TILE, tokens))
        bias = []
        for j in range(m):
            at = first + j * TILE
            allowed = (key + at).astype(jnp.float32) >= low
            if at + TILE > WINDOW:
                allowed = allowed & (key + (at - WINDOW) <= row)
            bias.append(jnp.where(allowed, 0.0, BELOW))
        bias = jnp.concatenate(bias, axis=0)
        span = pl.ds(first // ROWS, m * TILE // ROWS)

        def head(h, carry):
            at = lambda base: pl.ds(pl.multiple_of((base + h) * HEAD_DIM, HEAD_DIM), HEAD_DIM)
            q = q_ref[b, :, at(start)]
            k = held[span, :, at(0)].reshape(m * TILE, HEAD_DIM)
            v = held[span, :, at(heads)].reshape(m * TILE, HEAD_DIM)
            scores = bias + lax.dot_general(
                k, q, (((1,), (1,)), ((), ())), preferred_element_type=jnp.float32
            )
            row_max = jnp.max(scores, axis=0, keepdims=True)
            probs = jnp.exp2((scores - row_max) * scale)
            totals = jnp.sum(probs, axis=0, keepdims=True)
            mixed = lax.dot_general(
                v, probs.astype(jnp.bfloat16), (((0,), (0,)), ((), ())), preferred_element_type=jnp.float32
            )
            out_ref[b, :, at(out_start)] = (mixed / totals).T.astype(jnp.bfloat16)
            return carry

        if heads <= UNROLLED:
            for h in range(heads):
                head(h, 0)
        else:
            lax.fori_loop(0, heads, head, 0)

    def kernel(plan_ref, lows_ref, q_ref, local_ref, near_ref, far_ref, *others):
        out_ref, held = others[-2:]
        held[...] = jnp.zeros_like(held)

        def stretch(b, carry):
            held[halo:] = local_ref[b, :, : 2 * wide].reshape(chunk, ROWS, 2 * wide)
            for ref, at, end in ((near_ref, 0, halo), (far_ref, 2, halo - chunk)):
                first, count = plan_ref[at, b], plan_ref[at + 1, b]

                def move(j, carry, ref=ref, first=first, to=end - count):
                    held[to + j] = ref[first + j]
                    return carry

                lax.fori_loop(0, count, move, 0)

            need = plan_ref[4, b]
            for less, m in zip((0, *spans), spans):
                pl.when((need > less) & (need <= m))(functools.partial(attend, m, b, lows_ref, q_ref, out_ref, held))
            return carry

        lax.fori_loop(0, stretches, stretch, 0)

    return pl.pallas_call(
        kernel,
        out_shape=jax.ShapeDtypeStruct((stretches, tokens, out_heads * HEAD_DIM), query.dtype),
        in_specs=[pl.BlockSpec(memory_space=pltpu.SMEM)]
        + [pl.BlockSpec(memory_space=pltpu.VMEM)] * (5 if earlier is None else 6),
        input_output_aliases={} if earlier is None else {6: 0},
        out_specs=pl.BlockSpec(memory_space=pltpu.VMEM),
        scratch_shapes=[pltpu.VMEM((halo + chunk, ROWS, 2 * wide), jnp.bfloat16)],
        compiler_params=pltpu.CompilerParams(vmem_limit_bytes=32 * 1024 * 1024),
        cost_estimate=pl.CostEstimate(
            flops=4 * stretches * tokens * heads * HEAD_DIM * 3 * TILE,
            bytes_accessed=2 * (4 * stretches * tokens * wide + near.size + far.size),
            transcendentals=stretches * tokens * heads * 3 * TILE,
        ),
        name="attention",
    )(plan, lows, query, local, near, far, *(() if earlier is None else (earlier,)))


def shards(groups, ring, queries, keys, values, doc_start):
    tokens = queries.shape[0]
    group_heads = max(1, 3 * HEADS // (4 * groups))
    rest_heads = HEADS - groups * group_heads
    chunk = tokens // ROWS
    chunks = groups * ring
    plane = lax.axis_index("uly")
    me = lax.axis_index("blk") * ring + plane

    def spread(array):
        return lax.all_to_all(array, "blk", split_axis=0, concat_axis=0, tiled=True)

    def onward(array):
        return lax.ppermute(array, "uly", [(i, (i + 1) % ring) for i in range(ring)])

    def next_chunk(array):
        return lax.ppermute(array, ("blk", "uly"), [(i, i + 1) for i in range(chunks - 1)])

    wide, rest = group_heads * HEAD_DIM, rest_heads * HEAD_DIM
    own_pair = rest_of(keys, values, rest)
    own_next = next_chunk(own_pair)
    own_after = next_chunk(own_next)

    lanes = lax.optimization_barrier((doc_start, own_pair))[0].reshape(1, -1, 128)
    starts = spread(jnp.broadcast_to(lanes, (groups, *lanes.shape[1:])))
    by_chunk = starts.reshape(chunks, tokens)
    opens = jnp.arange(chunks, dtype=jnp.int32) * tokens
    need = jnp.minimum(opens - by_chunk[:, 0], WINDOW - 1)
    near_need = (jnp.minimum(need, tokens) + ROWS - 1) // ROWS
    far_need = (jnp.maximum(need - tokens, 0) + ROWS - 1) // ROWS
    near_sum = jnp.max(jnp.sum(near_need.reshape(groups, ring), axis=0))
    far_sum = jnp.max(jnp.sum(far_need.reshape(groups, ring), axis=0))

    def mine(per_chunk, ahead):
        padded = jnp.concatenate([per_chunk, jnp.zeros((ring,), jnp.int32)])
        rolled = lax.dynamic_slice_in_dim(padded, plane + ahead, chunks, 0)
        return rolled.reshape(groups, ring)[:, 0]

    def before(counts):
        earlier = jnp.arange(groups)[None, :] < jnp.arange(groups)[:, None]
        return jnp.sum(jnp.where(earlier, counts[None, :], 0), axis=1)

    near_in, far_in = mine(near_need, 0), mine(far_need, 0)
    near_out, far_out = mine(near_need, 1), mine(far_need, 1)
    near_first = before(near_in)
    own_first = jnp.arange(groups, dtype=jnp.int32) * chunk + chunk - near_out
    near_plan = jnp.stack([own_first, before(near_out), near_out])
    far_plan = jnp.stack([near_first + near_in - far_out, before(far_out), far_out])

    position = jnp.arange(chunks * tokens, dtype=jnp.int32).reshape(chunks, tokens)
    lows = jnp.maximum(by_chunk, position - (WINDOW - 1)) - (opens[:, None] - WINDOW)
    tile_need = (WINDOW + tokens - lows[:, 0] + TILE - 1) // TILE
    lows = lows.astype(jnp.float32)
    plane_lows = lax.dynamic_index_in_dim(lows.reshape(groups, ring, tokens), plane, 1)
    plan = jnp.stack([near_first, near_in, before(far_in), far_in, mine(tile_need, 0)])

    def own(per_chunk):
        return lax.dynamic_index_in_dim(per_chunk, me, 0, keepdims=False)

    own_near, own_far = own(near_need), own(far_need)
    own_plan = jnp.stack([chunk - own_near, own_near, chunk - own_far, own_far, own(tile_need)])[:, None]
    own_lows = own(lows)[None, None]

    lead = (group_heads + 1) // 2
    tail = group_heads - lead
    pair, = split_heads((keys, values), groups, group_heads, (((0, 0, lead), (1, 0, lead)),))
    pair = spread(pair)
    later = lax.optimization_barrier((keys, values, queries, starts))[:3]
    wanted = (((2, 0, lead),), ((2, 0, 0),)) + ((((0, lead, tail), (1, lead, tail), (2, lead, tail)),) if tail else ())
    query, own_query, *trio = split_heads(later, groups, group_heads, wanted)

    def run(room, pair, query, trio, near_plan, far_plan, plan, plane_lows, own_query, own_pair, own_next, own_after, own_plan, own_lows):
        near_slots, far_slots = (groups * chunk * share // 64 for share in room)
        as_blocks = lambda array: array.reshape(-1, ROWS, array.shape[2])
        tied = lambda array, *others: lax.optimization_barrier((array, others))[0]
        wide, narrow = 2 * lead * HEAD_DIM, 2 * tail * HEAD_DIM

        packed = pack(as_blocks(pair), near_plan, near_slots, wide)
        near = onward(packed)
        query = spread(tied(query, packed))
        if tail:
            (trio,) = (spread(tied(array, query)) for array in trio)
        own_out = attention(
            own_plan, own_lows, tied(own_query, packed), (0, rest_heads), own_pair,
            as_blocks(own_next), as_blocks(own_after),
        )
        near = tied(near, own_out)
        passed = pack(near, far_plan, far_slots, wide)
        far = onward(passed)
        if tail:
            ready = pack(as_blocks(tied(trio, passed)), near_plan, near_slots, narrow)
            near_tail = onward(ready)
        out = attention(plan, plane_lows, query, (0, lead), pair, near, far)
        done = [spread(out)]
        if tail:
            far_tail = onward(pack(tied(near_tail, out), far_plan, far_slots, narrow))
            out = attention(plan, plane_lows, trio, (2 * tail, tail), trio, near_tail, far_tail)
            done.append(spread(tied(out, done)))
        return done, own_out

    shares = [[groups * chunk * share // 64 for share in room] for room in ROOMS]
    level = sum(
        ((near_sum > near) | (far_sum > far)).astype(jnp.int32) for near, far in shares[:-1]
    )
    done, own_out = lax.switch(
        level, [functools.partial(run, room) for room in ROOMS],
        pair, query, trio, near_plan, far_plan, plan, plane_lows, own_query, own_pair, own_next, own_after, own_plan, own_lows,
    )
    return join_heads(done, own_out)


def solution(mesh):
    return jax.shard_map(
        functools.partial(shards, mesh.shape["blk"], mesh.shape["uly"]),
        mesh=mesh,
        in_specs=(
            P(("blk", "uly"), None),
            P(("blk", "uly"), None),
            P(("blk", "uly"), None),
            P("blk"),
        ),
        out_specs=P(("blk", "uly"), None),
        check_vma=False,
    )
```

```python
import functools
import math

import jax
import jax.numpy as jnp
from jax import lax
from jax.experimental import pallas as pl
from jax.experimental.pallas import tpu as pltpu
from jax.sharding import PartitionSpec as P

HEADS = 32
HEAD_DIM = 128
WINDOW = 512
TILE = 128
ROWS = 16
BELOW = -1e30
HINT = 2 * 10**10
UNROLLED = 3
ROOMS = ((66, 20), (72, 34), (86, 36), (100, 56), (128, 128))


def split_heads(sources, groups, group_heads, wanted):
    tokens, columns = sources[0].shape
    band = group_heads * HEAD_DIM
    rest = columns - groups * band
    rows = min(64, tokens)
    shapes = [
        (groups if parts[0][2] else 1, rows, sum(size * HEAD_DIM or rest for _, _, size in parts))
        for parts in wanted
    ]

    def kernel(*refs):
        for out, parts in zip(refs[len(sources) :], wanted):
            to = 0
            for which, start, size in parts:
                wide = size * HEAD_DIM or rest
                for g in range(groups if size else 1):
                    first = g * band + start * HEAD_DIM if size else groups * band
                    out[g, :, to : to + wide] = refs[which][:, first : first + wide]
                to += wide

    return pl.pallas_call(
        kernel,
        grid=(tokens // rows,),
        out_shape=[
            jax.ShapeDtypeStruct((shape[0], tokens, shape[2]), sources[0].dtype) for shape in shapes
        ],
        in_specs=[pl.BlockSpec((rows, columns), lambda t: (t, 0))] * len(sources),
        out_specs=[pl.BlockSpec(shape, lambda t: (0, t, 0)) for shape in shapes],
        cost_estimate=pl.CostEstimate(
            flops=0, bytes_accessed=4 * len(sources) * sources[0].size, transcendentals=0
        ),
        name="split_heads",
    )(*sources)


def rest_of(keys, values, rest):
    tokens, columns = keys.shape
    rows = min(128, tokens)

    def kernel(k_ref, v_ref, out_ref):
        out_ref[0, :, :rest] = k_ref[...]
        out_ref[0, :, rest:] = v_ref[...]

    return pl.pallas_call(
        kernel,
        grid=(tokens // rows,),
        out_shape=jax.ShapeDtypeStruct((1, tokens, 2 * rest), keys.dtype),
        in_specs=[pl.BlockSpec((rows, rest), lambda t: (t, columns // rest - 1))] * 2,
        out_specs=pl.BlockSpec((1, rows, 2 * rest), lambda t: (0, t, 0)),
        cost_estimate=pl.CostEstimate(flops=0, bytes_accessed=8 * tokens * rest, transcendentals=0),
        name="rest_of",
    )(keys, values)


def join_heads(pieces, rest):
    groups, tokens, _ = pieces[0].shape
    band = sum(piece.shape[2] for piece in pieces)
    rows = min(64, tokens)

    def kernel(*refs):
        ins, other, out = refs[:-2], refs[-2], refs[-1]
        for g in range(groups):
            first = g * band
            for src in ins:
                out[:, first : first + src.shape[2]] = src[g]
                first += src.shape[2]
        out[:, groups * band :] = other[0]

    columns = groups * band + rest.shape[2]
    return pl.pallas_call(
        kernel,
        grid=(tokens // rows,),
        out_shape=jax.ShapeDtypeStruct((tokens, columns), rest.dtype),
        in_specs=[
            pl.BlockSpec((piece.shape[0], rows, piece.shape[2]), lambda t: (0, t, 0))
            for piece in (*pieces, rest)
        ],
        out_specs=pl.BlockSpec((rows, columns), lambda t: (t, 0)),
        cost_estimate=pl.CostEstimate(flops=0, bytes_accessed=4 * tokens * columns, transcendentals=0),
        name="join_heads",
    )(*pieces, rest)


def pack(blocks, plan, slots, wide, hint=0):
    rows = blocks.shape[1]
    stretches = plan.shape[1]

    def kernel(plan_ref, in_ref, out_ref):
        def stretch(b, carry):
            src, dst, count = plan_ref[0, b], plan_ref[1, b], plan_ref[2, b]

            def move(j, carry):
                out_ref[dst + j] = in_ref[src + j, :, :wide]
                return carry

            return lax.fori_loop(0, count, move, carry)

        lax.fori_loop(0, stretches, stretch, 0)

    return pl.pallas_call(
        kernel,
        out_shape=jax.ShapeDtypeStruct((slots, rows, wide), blocks.dtype),
        in_specs=[pl.BlockSpec(memory_space=pltpu.SMEM), pl.BlockSpec(memory_space=pltpu.VMEM)],
        out_specs=pl.BlockSpec(memory_space=pltpu.VMEM),
        compiler_params=pltpu.CompilerParams(vmem_limit_bytes=32 * 1024 * 1024),
        cost_estimate=pl.CostEstimate(
            flops=hint, bytes_accessed=4 * slots * rows * wide, transcendentals=0
        ),
        name="pack_halo",
    )(plan, blocks)


def attention(plan, lows, query, query_heads, local, near, far, earlier=None, out_at=(0, None)):
    start, heads = query_heads
    out_start, out_heads = out_at[0], out_at[1] or heads
    stretches, tokens, _ = query.shape
    wide = heads * HEAD_DIM
    least, most = tokens // TILE, (WINDOW + tokens) // TILE
    spans = (*range(least, most - 1), most)
    halo = WINDOW // ROWS
    chunk = tokens // ROWS
    scale = math.log2(math.e) / math.sqrt(HEAD_DIM)

    def attend(m, b, lows_ref, q_ref, out_ref, held):
        first = WINDOW + tokens - m * TILE
        key = lax.broadcasted_iota(jnp.int32, (TILE, tokens), 0)
        row = lax.broadcasted_iota(jnp.int32, (TILE, tokens), 1)
        low = jnp.broadcast_to(lows_ref[b], (TILE, tokens))
        bias = []
        for j in range(m):
            at = first + j * TILE
            allowed = (key + at).astype(jnp.float32) >= low
            if at + TILE > WINDOW:
                allowed = allowed & (key + (at - WINDOW) <= row)
            bias.append(jnp.where(allowed, 0.0, BELOW))
        bias = jnp.concatenate(bias, axis=0)
        span = pl.ds(first // ROWS, m * TILE // ROWS)

        def head(h, carry):
            at = lambda base: pl.ds(pl.multiple_of((base + h) * HEAD_DIM, HEAD_DIM), HEAD_DIM)
            q = q_ref[b, :, at(start)]
            k = held[span, :, at(0)].reshape(m * TILE, HEAD_DIM)
            v = held[span, :, at(heads)].reshape(m * TILE, HEAD_DIM)
            scores = bias + lax.dot_general(
                k, q, (((1,), (1,)), ((), ())), preferred_element_type=jnp.float32
            )
            row_max = jnp.max(scores, axis=0, keepdims=True)
            probs = jnp.exp2((scores - row_max) * scale)
            totals = jnp.sum(probs, axis=0, keepdims=True)
            mixed = lax.dot_general(
                v, probs.astype(jnp.bfloat16), (((0,), (0,)), ((), ())), preferred_element_type=jnp.float32
            )
            out_ref[b, :, at(out_start)] = (mixed / totals).T.astype(jnp.bfloat16)
            return carry

        if heads <= UNROLLED:
            for h in range(heads):
                head(h, 0)
        else:
            lax.fori_loop(0, heads, head, 0)

    def kernel(plan_ref, lows_ref, q_ref, local_ref, near_ref, far_ref, *others):
        out_ref, held = others[-2:]
        held[...] = jnp.zeros_like(held)

        def stretch(b, carry):
            held[halo:] = local_ref[b, :, : 2 * wide].reshape(chunk, ROWS, 2 * wide)
            for ref, at, end in ((near_ref, 0, halo), (far_ref, 2, halo - chunk)):
                first, count = plan_ref[at, b], plan_ref[at + 1, b]

                def move(j, carry, ref=ref, first=first, to=end - count):
                    held[to + j] = ref[first + j]
                    return carry

                lax.fori_loop(0, count, move, 0)

            need = plan_ref[4, b]
            for less, m in zip((0, *spans), spans):
                pl.when((need > less) & (need <= m))(functools.partial(attend, m, b, lows_ref, q_ref, out_ref, held))
            return carry

        lax.fori_loop(0, stretches, stretch, 0)

    return pl.pallas_call(
        kernel,
        out_shape=jax.ShapeDtypeStruct((stretches, tokens, out_heads * HEAD_DIM), query.dtype),
        in_specs=[pl.BlockSpec(memory_space=pltpu.SMEM)]
        + [pl.BlockSpec(memory_space=pltpu.VMEM)] * (5 if earlier is None else 6),
        input_output_aliases={} if earlier is None else {6: 0},
        out_specs=pl.BlockSpec(memory_space=pltpu.VMEM),
        scratch_shapes=[pltpu.VMEM((halo + chunk, ROWS, 2 * wide), jnp.bfloat16)],
        compiler_params=pltpu.CompilerParams(vmem_limit_bytes=32 * 1024 * 1024),
        cost_estimate=pl.CostEstimate(
            flops=4 * stretches * tokens * heads * HEAD_DIM * 3 * TILE,
            bytes_accessed=2 * (4 * stretches * tokens * wide + near.size + far.size),
            transcendentals=stretches * tokens * heads * 3 * TILE,
        ),
        name="attention",
    )(plan, lows, query, local, near, far, *(() if earlier is None else (earlier,)))


def shards(groups, ring, queries, keys, values, doc_start):
    tokens = queries.shape[0]
    group_heads = max(1, 3 * HEADS // (4 * groups))
    rest_heads = HEADS - groups * group_heads
    chunk = tokens // ROWS
    chunks = groups * ring
    plane = lax.axis_index("uly")
    me = lax.axis_index("blk") * ring + plane

    def spread(array):
        return lax.all_to_all(array, "blk", split_axis=0, concat_axis=0, tiled=True)

    def onward(array):
        return lax.ppermute(array, "uly", [(i, (i + 1) % ring) for i in range(ring)])

    def next_chunk(array):
        return lax.ppermute(array, ("blk", "uly"), [(i, i + 1) for i in range(chunks - 1)])

    wide, rest = group_heads * HEAD_DIM, rest_heads * HEAD_DIM
    own_pair = rest_of(keys, values, rest)
    own_next = next_chunk(own_pair)
    own_after = next_chunk(own_next)

    lanes = lax.optimization_barrier((doc_start, own_pair))[0].reshape(1, -1, 128)
    starts = spread(jnp.broadcast_to(lanes, (groups, *lanes.shape[1:])))
    by_chunk = starts.reshape(chunks, tokens)
    opens = jnp.arange(chunks, dtype=jnp.int32) * tokens
    need = jnp.minimum(opens - by_chunk[:, 0], WINDOW - 1)
    near_need = (jnp.minimum(need, tokens) + ROWS - 1) // ROWS
    far_need = (jnp.maximum(need - tokens, 0) + ROWS - 1) // ROWS
    near_sum = jnp.max(jnp.sum(near_need.reshape(groups, ring), axis=0))
    far_sum = jnp.max(jnp.sum(far_need.reshape(groups, ring), axis=0))

    def mine(per_chunk, ahead):
        padded = jnp.concatenate([per_chunk, jnp.zeros((ring,), jnp.int32)])
        rolled = lax.dynamic_slice_in_dim(padded, plane + ahead, chunks, 0)
        return rolled.reshape(groups, ring)[:, 0]

    def before(counts):
        earlier = jnp.arange(groups)[None, :] < jnp.arange(groups)[:, None]
        return jnp.sum(jnp.where(earlier, counts[None, :], 0), axis=1)

    near_in, far_in = mine(near_need, 0), mine(far_need, 0)
    near_out, far_out = mine(near_need, 1), mine(far_need, 1)
    near_first = before(near_in)
    own_first = jnp.arange(groups, dtype=jnp.int32) * chunk + chunk - near_out
    near_plan = jnp.stack([own_first, before(near_out), near_out])
    far_plan = jnp.stack([near_first + near_in - far_out, before(far_out), far_out])

    position = jnp.arange(chunks * tokens, dtype=jnp.int32).reshape(chunks, tokens)
    lows = jnp.maximum(by_chunk, position - (WINDOW - 1)) - (opens[:, None] - WINDOW)
    tile_need = (WINDOW + tokens - lows[:, 0] + TILE - 1) // TILE
    lows = lows.astype(jnp.float32)
    plane_lows = lax.dynamic_index_in_dim(lows.reshape(groups, ring, tokens), plane, 1)
    plan = jnp.stack([near_first, near_in, before(far_in), far_in, mine(tile_need, 0)])

    def own(per_chunk):
        return lax.dynamic_index_in_dim(per_chunk, me, 0, keepdims=False)

    own_near, own_far = own(near_need), own(far_need)
    own_plan = jnp.stack([chunk - own_near, own_near, chunk - own_far, own_far, own(tile_need)])[:, None]
    own_lows = own(lows)[None, None]

    lead = (group_heads + 1) // 2
    tail = group_heads - lead
    pair, = split_heads((keys, values), groups, group_heads, (((0, 0, lead), (1, 0, lead)),))
    pair = spread(pair)
    later = lax.optimization_barrier((keys, values, queries, starts))[:3]
    wanted = (((2, 0, lead),), ((2, 0, 0),)) + ((((0, lead, tail), (1, lead, tail), (2, lead, tail)),) if tail else ())
    query, own_query, *trio = split_heads(later, groups, group_heads, wanted)

    def run(room, pair, query, trio, near_plan, far_plan, plan, plane_lows, own_query, own_pair, own_next, own_after, own_plan, own_lows):
        near_slots, far_slots = (groups * chunk * share // 128 for share in room)
        as_blocks = lambda array: array.reshape(-1, ROWS, array.shape[2])
        tied = lambda array, *others: lax.optimization_barrier((array, others))[0]
        wide, narrow = 2 * lead * HEAD_DIM, 2 * tail * HEAD_DIM

        packed = pack(as_blocks(pair), near_plan, near_slots, wide)
        near = onward(packed)
        query = spread(tied(query, packed))
        if tail:
            (trio,) = (spread(tied(array, query)) for array in trio)
        passed = pack(near, far_plan, far_slots, wide, HINT)
        far = onward(passed)
        if tail:
            ready = pack(as_blocks(tied(trio, far)), near_plan, near_slots, narrow)
            near_tail = onward(ready)
            far = tied(far, ready)
        out = attention(plan, plane_lows, query, (0, lead), pair, near, far)
        if tail:
            passed = pack(tied(near_tail, out), far_plan, far_slots, narrow, HINT)
            far_tail = onward(passed)
        done = [spread(out)]
        own_query = tied(own_query, passed, out)
        own_out = attention(
            own_plan, own_lows, own_query, (0, rest_heads), own_pair,
            as_blocks(own_next), as_blocks(own_after),
        )
        if tail:
            far_tail = tied(far_tail, own_out)
            out = attention(plan, plane_lows, trio, (2 * tail, tail), trio, near_tail, far_tail)
            done.append(spread(tied(out, done)))
        return done, own_out

    shares = [[groups * chunk * share // 128 for share in room] for room in ROOMS]
    level = sum(
        ((near_sum > near) | (far_sum > far)).astype(jnp.int32) for near, far in shares[:-1]
    )
    done, own_out = lax.switch(
        level, [functools.partial(run, room) for room in ROOMS],
        pair, query, trio, near_plan, far_plan, plan, plane_lows, own_query, own_pair, own_next, own_after, own_plan, own_lows,
    )
    return join_heads(done, own_out)


def solution(mesh):
    return jax.shard_map(
        functools.partial(shards, mesh.shape["blk"], mesh.shape["uly"]),
        mesh=mesh,
        in_specs=(
            P(("blk", "uly"), None),
            P(("blk", "uly"), None),
            P(("blk", "uly"), None),
            P("blk"),
        ),
        out_specs=P(("blk", "uly"), None),
        check_vma=False,
    )
```

```python
import functools
import math

import jax
import jax.numpy as jnp
from jax import lax
from jax.experimental import pallas as pl
from jax.experimental.pallas import tpu as pltpu
from jax.sharding import PartitionSpec as P

HEADS = 32
HEAD_DIM = 128
WINDOW = 512
TILE = 128
ROWS = 16
BELOW = -1e30
HINT = 2 * 10**10
UNROLLED = 3
ROOMS = ((72, 25), (86, 36), (98, 49), (106, 71), (128, 128))


def split_heads(sources, groups, group_heads, wanted):
    tokens, columns = sources[0].shape
    band = group_heads * HEAD_DIM
    rest = columns - groups * band
    rows = min(64, tokens)
    shapes = [
        (groups if parts[0][2] else 1, rows, sum(size * HEAD_DIM or rest for _, _, size in parts))
        for parts in wanted
    ]

    def kernel(*refs):
        for out, parts in zip(refs[len(sources) :], wanted):
            to = 0
            for which, start, size in parts:
                wide = size * HEAD_DIM or rest
                for g in range(groups if size else 1):
                    first = g * band + start * HEAD_DIM if size else groups * band
                    out[g, :, to : to + wide] = refs[which][:, first : first + wide]
                to += wide

    return pl.pallas_call(
        kernel,
        grid=(tokens // rows,),
        out_shape=[
            jax.ShapeDtypeStruct((shape[0], tokens, shape[2]), sources[0].dtype) for shape in shapes
        ],
        in_specs=[pl.BlockSpec((rows, columns), lambda t: (t, 0))] * len(sources),
        out_specs=[pl.BlockSpec(shape, lambda t: (0, t, 0)) for shape in shapes],
        cost_estimate=pl.CostEstimate(
            flops=0, bytes_accessed=4 * len(sources) * sources[0].size, transcendentals=0
        ),
        name="split_heads",
    )(*sources)


def rest_of(keys, values, rest):
    tokens, columns = keys.shape
    rows = min(128, tokens)

    def kernel(k_ref, v_ref, out_ref):
        out_ref[0, :, :rest] = k_ref[...]
        out_ref[0, :, rest:] = v_ref[...]

    return pl.pallas_call(
        kernel,
        grid=(tokens // rows,),
        out_shape=jax.ShapeDtypeStruct((1, tokens, 2 * rest), keys.dtype),
        in_specs=[pl.BlockSpec((rows, rest), lambda t: (t, columns // rest - 1))] * 2,
        out_specs=pl.BlockSpec((1, rows, 2 * rest), lambda t: (0, t, 0)),
        cost_estimate=pl.CostEstimate(flops=0, bytes_accessed=8 * tokens * rest, transcendentals=0),
        name="rest_of",
    )(keys, values)


def join_heads(pieces, rest):
    groups, tokens, _ = pieces[0].shape
    band = sum(piece.shape[2] for piece in pieces)
    rows = min(64, tokens)

    def kernel(*refs):
        ins, other, out = refs[:-2], refs[-2], refs[-1]
        for g in range(groups):
            first = g * band
            for src in ins:
                out[:, first : first + src.shape[2]] = src[g]
                first += src.shape[2]
        out[:, groups * band :] = other[0]

    columns = groups * band + rest.shape[2]
    return pl.pallas_call(
        kernel,
        grid=(tokens // rows,),
        out_shape=jax.ShapeDtypeStruct((tokens, columns), rest.dtype),
        in_specs=[
            pl.BlockSpec((piece.shape[0], rows, piece.shape[2]), lambda t: (0, t, 0))
            for piece in (*pieces, rest)
        ],
        out_specs=pl.BlockSpec((rows, columns), lambda t: (t, 0)),
        cost_estimate=pl.CostEstimate(flops=0, bytes_accessed=4 * tokens * columns, transcendentals=0),
        name="join_heads",
    )(*pieces, rest)


def pack(blocks, plan, slots, wide, hint=0):
    rows = blocks.shape[1]
    stretches = plan.shape[1]

    def kernel(plan_ref, in_ref, out_ref):
        def stretch(b, carry):
            src, dst, count = plan_ref[0, b], plan_ref[1, b], plan_ref[2, b]

            def move(j, carry):
                out_ref[dst + j] = in_ref[src + j, :, :wide]
                return carry

            return lax.fori_loop(0, count, move, carry)

        lax.fori_loop(0, stretches, stretch, 0)

    return pl.pallas_call(
        kernel,
        out_shape=jax.ShapeDtypeStruct((slots, rows, wide), blocks.dtype),
        in_specs=[pl.BlockSpec(memory_space=pltpu.SMEM), pl.BlockSpec(memory_space=pltpu.VMEM)],
        out_specs=pl.BlockSpec(memory_space=pltpu.VMEM),
        compiler_params=pltpu.CompilerParams(vmem_limit_bytes=32 * 1024 * 1024),
        cost_estimate=pl.CostEstimate(
            flops=hint, bytes_accessed=4 * slots * rows * wide, transcendentals=0
        ),
        name="pack_halo",
    )(plan, blocks)


def attention(plan, lows, query, query_heads, local, near, far, spans):
    start, heads = query_heads
    stretches, tokens, _ = query.shape
    wide = heads * HEAD_DIM
    halo = WINDOW // ROWS
    chunk = tokens // ROWS
    scale = math.log2(math.e) / math.sqrt(HEAD_DIM)

    def attend(m, b, lows_ref, q_ref, out_ref, held):
        first = WINDOW + tokens - m * TILE
        key = lax.broadcasted_iota(jnp.int32, (TILE, tokens), 0)
        row = lax.broadcasted_iota(jnp.int32, (TILE, tokens), 1)
        low = jnp.broadcast_to(lows_ref[b], (TILE, tokens))
        bias = []
        for j in range(m):
            at = first + j * TILE
            allowed = (key + at).astype(jnp.float32) >= low
            if at + TILE > WINDOW:
                allowed = allowed & (key + (at - WINDOW) <= row)
            bias.append(jnp.where(allowed, 0.0, BELOW))
        bias = jnp.concatenate(bias, axis=0)
        span = pl.ds(first // ROWS, m * TILE // ROWS)

        def head(h, carry):
            at = lambda base: pl.ds(pl.multiple_of((base + h) * HEAD_DIM, HEAD_DIM), HEAD_DIM)
            q = q_ref[b, :, at(start)]
            k = held[span, :, at(0)].reshape(m * TILE, HEAD_DIM)
            v = held[span, :, at(heads)].reshape(m * TILE, HEAD_DIM)
            scores = bias + lax.dot_general(
                k, q, (((1,), (1,)), ((), ())), preferred_element_type=jnp.float32
            )
            row_max = jnp.max(scores, axis=0, keepdims=True)
            probs = jnp.exp2((scores - row_max) * scale)
            totals = jnp.sum(probs, axis=0, keepdims=True)
            mixed = lax.dot_general(
                v, probs.astype(jnp.bfloat16), (((0,), (0,)), ((), ())), preferred_element_type=jnp.float32
            )
            out_ref[b, :, at(0)] = (mixed / totals).T.astype(jnp.bfloat16)
            return carry

        if heads <= UNROLLED:
            for h in range(heads):
                head(h, 0)
        else:
            lax.fori_loop(0, heads, head, 0)

    def kernel(plan_ref, lows_ref, q_ref, local_ref, near_ref, far_ref, out_ref, held):
        held[...] = jnp.zeros_like(held)

        def stretch(b, carry):
            held[halo:] = local_ref[b, :, : 2 * wide].reshape(chunk, ROWS, 2 * wide)
            for ref, at, end in ((near_ref, 0, halo), (far_ref, 2, halo - chunk)):
                first, count = plan_ref[at, b], plan_ref[at + 1, b]

                def move(j, carry, ref=ref, first=first, to=end - count):
                    held[to + j] = ref[first + j]
                    return carry

                lax.fori_loop(0, count, move, 0)

            need = plan_ref[4, b]
            for less, m in zip((0, *spans), spans):
                pl.when((need > less) & (need <= m))(functools.partial(attend, m, b, lows_ref, q_ref, out_ref, held))
            return carry

        lax.fori_loop(0, stretches, stretch, 0)

    return pl.pallas_call(
        kernel,
        out_shape=jax.ShapeDtypeStruct((stretches, tokens, wide), query.dtype),
        in_specs=[pl.BlockSpec(memory_space=pltpu.SMEM)] + [pl.BlockSpec(memory_space=pltpu.VMEM)] * 5,
        out_specs=pl.BlockSpec(memory_space=pltpu.VMEM),
        scratch_shapes=[pltpu.VMEM((halo + chunk, ROWS, 2 * wide), jnp.bfloat16)],
        compiler_params=pltpu.CompilerParams(vmem_limit_bytes=32 * 1024 * 1024),
        cost_estimate=pl.CostEstimate(
            flops=4 * stretches * tokens * heads * HEAD_DIM * 3 * TILE,
            bytes_accessed=2 * (4 * stretches * tokens * wide + near.size + far.size),
            transcendentals=stretches * tokens * heads * 3 * TILE,
        ),
        name="attention",
    )(plan, lows, query, local, near, far)


def shards(groups, ring, queries, keys, values, doc_start):
    tokens = queries.shape[0]
    group_heads = max(1, 3 * HEADS // (4 * groups))
    rest_heads = HEADS - groups * group_heads
    chunk = tokens // ROWS
    chunks = groups * ring
    plane = lax.axis_index("uly")
    me = lax.axis_index("blk") * ring + plane

    def spread(array):
        return lax.all_to_all(array, "blk", split_axis=0, concat_axis=0, tiled=True)

    def onward(array):
        return lax.ppermute(array, "uly", [(i, (i + 1) % ring) for i in range(ring)])

    def next_chunk(array):
        return lax.ppermute(array, ("blk", "uly"), [(i, i + 1) for i in range(chunks - 1)])

    wide, rest = group_heads * HEAD_DIM, rest_heads * HEAD_DIM
    own_pair = rest_of(keys, values, rest)
    own_next = next_chunk(own_pair)
    own_after = next_chunk(own_next)

    lanes = lax.optimization_barrier((doc_start, own_pair))[0].reshape(1, -1, 128)
    starts = spread(jnp.broadcast_to(lanes, (groups, *lanes.shape[1:])))
    by_chunk = starts.reshape(chunks, tokens)
    opens = jnp.arange(chunks, dtype=jnp.int32) * tokens
    need = jnp.minimum(opens - by_chunk[:, 0], WINDOW - 1)
    near_need = (jnp.minimum(need, tokens) + ROWS - 1) // ROWS
    far_need = (jnp.maximum(need - tokens, 0) + ROWS - 1) // ROWS
    near_sum = jnp.max(jnp.sum(near_need.reshape(groups, ring), axis=0))
    far_sum = jnp.max(jnp.sum(far_need.reshape(groups, ring), axis=0))

    def mine(per_chunk, ahead):
        padded = jnp.concatenate([per_chunk, jnp.zeros((ring,), jnp.int32)])
        rolled = lax.dynamic_slice_in_dim(padded, plane + ahead, chunks, 0)
        return rolled.reshape(groups, ring)[:, 0]

    def before(counts):
        earlier = jnp.arange(groups)[None, :] < jnp.arange(groups)[:, None]
        return jnp.sum(jnp.where(earlier, counts[None, :], 0), axis=1)

    near_in, far_in = mine(near_need, 0), mine(far_need, 0)
    near_out, far_out = mine(near_need, 1), mine(far_need, 1)
    near_first = before(near_in)
    own_first = jnp.arange(groups, dtype=jnp.int32) * chunk + chunk - near_out
    near_plan = jnp.stack([own_first, before(near_out), near_out])
    far_plan = jnp.stack([near_first + near_in - far_out, before(far_out), far_out])

    position = jnp.arange(chunks * tokens, dtype=jnp.int32).reshape(chunks, tokens)
    lows = jnp.maximum(by_chunk, position - (WINDOW - 1)) - (opens[:, None] - WINDOW)
    tile_need = (WINDOW + tokens - lows[:, 0] + TILE - 1) // TILE
    lows = lows.astype(jnp.float32)
    plane_lows = lax.dynamic_index_in_dim(lows.reshape(groups, ring, tokens), plane, 1)
    plan = jnp.stack([near_first, near_in, before(far_in), far_in, mine(tile_need, 0)])

    def own(per_chunk):
        return lax.dynamic_index_in_dim(per_chunk, me, 0, keepdims=False)

    own_near, own_far = own(near_need), own(far_need)
    own_plan = jnp.stack([chunk - own_near, own_near, chunk - own_far, own_far, own(tile_need)])[:, None]
    own_lows = own(lows)[None, None]

    lead = (group_heads + 1) // 2
    tail = group_heads - lead
    pair, = split_heads((keys, values), groups, group_heads, (((0, 0, lead), (1, 0, lead)),))
    pair = spread(pair)
    most = (WINDOW + tokens) // TILE
    spans = (most - 3, most - 2, most)
    later = lax.optimization_barrier((keys, values, queries, starts))[:3]
    wanted = (((2, 0, lead),), ((2, 0, 0),)) + ((((0, lead, tail), (1, lead, tail), (2, lead, tail)),) if tail else ())
    query, own_query, *trio = split_heads(later, groups, group_heads, wanted)

    def run(room, pair, query, trio, near_plan, far_plan, plan, plane_lows, own_query, own_pair, own_next, own_after, own_plan, own_lows):
        near_slots, far_slots = (groups * chunk * share // 128 for share in room)
        as_blocks = lambda array: array.reshape(-1, ROWS, array.shape[2])
        tied = lambda array, *others: lax.optimization_barrier((array, others))[0]
        wide, narrow = 2 * lead * HEAD_DIM, 2 * tail * HEAD_DIM

        packed = pack(as_blocks(pair), near_plan, near_slots, wide)
        near = onward(packed)
        query = spread(tied(query, packed))
        if tail:
            (trio,) = (spread(tied(array, query)) for array in trio)
        passed = pack(near, far_plan, far_slots, wide, HINT)
        far = onward(passed)
        if tail:
            ready = pack(as_blocks(tied(trio, far)), near_plan, near_slots, narrow)
            near_tail = onward(ready)
            far = tied(far, ready)
        out = attention(plan, plane_lows, query, (0, lead), pair, near, far, spans)
        if tail:
            passed = pack(tied(near_tail, out), far_plan, far_slots, narrow, HINT)
            far_tail = onward(passed)
        done = [spread(out)]
        own_query = tied(own_query, passed, out)
        own_out = attention(
            own_plan, own_lows, own_query, (0, rest_heads), own_pair,
            as_blocks(own_next), as_blocks(own_after), spans[1:],
        )
        if tail:
            far_tail = tied(far_tail, own_out)
            out = attention(plan, plane_lows, trio, (2 * tail, tail), trio, near_tail, far_tail, spans)
            done.append(spread(tied(out, done)))
        return done, own_out

    shares = [[groups * chunk * share // 128 for share in room] for room in ROOMS]
    level = sum(
        ((near_sum > near) | (far_sum > far)).astype(jnp.int32) for near, far in shares[:-1]
    )
    done, own_out = lax.switch(
        level, [functools.partial(run, room) for room in ROOMS],
        pair, query, trio, near_plan, far_plan, plan, plane_lows, own_query, own_pair, own_next, own_after, own_plan, own_lows,
    )
    return join_heads(done, own_out)


def solution(mesh):
    return jax.shard_map(
        functools.partial(shards, mesh.shape["blk"], mesh.shape["uly"]),
        mesh=mesh,
        in_specs=(
            P(("blk", "uly"), None),
            P(("blk", "uly"), None),
            P(("blk", "uly"), None),
            P("blk"),
        ),
        out_specs=P(("blk", "uly"), None),
        check_vma=False,
    )
```

```python
import functools
import math

import jax
import jax.numpy as jnp
from jax import lax
from jax.experimental import pallas as pl
from jax.experimental.pallas import tpu as pltpu
from jax.sharding import PartitionSpec as P

HEADS = 32
HEAD_DIM = 128
WINDOW = 512
TILE = 128
ROWS = 16
BELOW = -1e30
HINT = 2 * 10**10
UNROLLED = 3
ROOMS = ((72, 22), (75, 35), (86, 36), (91, 49), (102, 66), (128, 128))


def split_heads(sources, groups, group_heads, wanted):
    tokens, columns = sources[0].shape
    band = group_heads * HEAD_DIM
    rest = columns - groups * band
    rows = min(64, tokens)
    shapes = [
        (groups if parts[0][2] else 1, rows, sum(size * HEAD_DIM or rest for _, _, size in parts))
        for parts in wanted
    ]

    def kernel(*refs):
        for out, parts in zip(refs[len(sources) :], wanted):
            to = 0
            for which, start, size in parts:
                wide = size * HEAD_DIM or rest
                for g in range(groups if size else 1):
                    first = g * band + start * HEAD_DIM if size else groups * band
                    out[g, :, to : to + wide] = refs[which][:, first : first + wide]
                to += wide

    return pl.pallas_call(
        kernel,
        grid=(tokens // rows,),
        out_shape=[
            jax.ShapeDtypeStruct((shape[0], tokens, shape[2]), sources[0].dtype) for shape in shapes
        ],
        in_specs=[pl.BlockSpec((rows, columns), lambda t: (t, 0))] * len(sources),
        out_specs=[pl.BlockSpec(shape, lambda t: (0, t, 0)) for shape in shapes],
        cost_estimate=pl.CostEstimate(
            flops=0, bytes_accessed=4 * len(sources) * sources[0].size, transcendentals=0
        ),
        name="split_heads",
    )(*sources)


def rest_of(keys, values, rest):
    tokens, columns = keys.shape
    rows = min(128, tokens)

    def kernel(k_ref, v_ref, out_ref):
        out_ref[0, :, :rest] = k_ref[...]
        out_ref[0, :, rest:] = v_ref[...]

    return pl.pallas_call(
        kernel,
        grid=(tokens // rows,),
        out_shape=jax.ShapeDtypeStruct((1, tokens, 2 * rest), keys.dtype),
        in_specs=[pl.BlockSpec((rows, rest), lambda t: (t, columns // rest - 1))] * 2,
        out_specs=pl.BlockSpec((1, rows, 2 * rest), lambda t: (0, t, 0)),
        cost_estimate=pl.CostEstimate(flops=0, bytes_accessed=8 * tokens * rest, transcendentals=0),
        name="rest_of",
    )(keys, values)


def join_heads(pieces, rest):
    groups, tokens, _ = pieces[0].shape
    band = sum(piece.shape[2] for piece in pieces)
    rows = min(64, tokens)

    def kernel(*refs):
        ins, other, out = refs[:-2], refs[-2], refs[-1]
        for g in range(groups):
            first = g * band
            for src in ins:
                out[:, first : first + src.shape[2]] = src[g]
                first += src.shape[2]
        out[:, groups * band :] = other[0]

    columns = groups * band + rest.shape[2]
    return pl.pallas_call(
        kernel,
        grid=(tokens // rows,),
        out_shape=jax.ShapeDtypeStruct((tokens, columns), rest.dtype),
        in_specs=[
            pl.BlockSpec((piece.shape[0], rows, piece.shape[2]), lambda t: (0, t, 0))
            for piece in (*pieces, rest)
        ],
        out_specs=pl.BlockSpec((rows, columns), lambda t: (t, 0)),
        cost_estimate=pl.CostEstimate(flops=0, bytes_accessed=4 * tokens * columns, transcendentals=0),
        name="join_heads",
    )(*pieces, rest)


def pack(blocks, plan, slots, wide, hint=0):
    rows = blocks.shape[1]
    stretches = plan.shape[1]

    def kernel(plan_ref, in_ref, out_ref):
        def stretch(b, carry):
            src, dst, count = plan_ref[0, b], plan_ref[1, b], plan_ref[2, b]

            def move(j, carry):
                out_ref[dst + j] = in_ref[src + j, :, :wide]
                return carry

            return lax.fori_loop(0, count, move, carry)

        lax.fori_loop(0, stretches, stretch, 0)

    return pl.pallas_call(
        kernel,
        out_shape=jax.ShapeDtypeStruct((slots, rows, wide), blocks.dtype),
        in_specs=[pl.BlockSpec(memory_space=pltpu.SMEM), pl.BlockSpec(memory_space=pltpu.VMEM)],
        out_specs=pl.BlockSpec(memory_space=pltpu.VMEM),
        compiler_params=pltpu.CompilerParams(vmem_limit_bytes=32 * 1024 * 1024),
        cost_estimate=pl.CostEstimate(
            flops=hint, bytes_accessed=4 * slots * rows * wide, transcendentals=0
        ),
        name="pack_halo",
    )(plan, blocks)


def attention(plan, lows, query, query_heads, local, near, far, spans):
    start, heads = query_heads
    stretches, tokens, _ = query.shape
    wide = heads * HEAD_DIM
    halo = WINDOW // ROWS
    chunk = tokens // ROWS
    scale = math.log2(math.e) / math.sqrt(HEAD_DIM)

    def attend(m, b, lows_ref, q_ref, out_ref, held):
        first = WINDOW + tokens - m * TILE
        key = lax.broadcasted_iota(jnp.int32, (TILE, tokens), 0)
        row = lax.broadcasted_iota(jnp.int32, (TILE, tokens), 1)
        low = jnp.broadcast_to(lows_ref[b], (TILE, tokens))
        bias = []
        for j in range(m):
            at = first + j * TILE
            allowed = (key + at).astype(jnp.float32) >= low
            if at + TILE > WINDOW:
                allowed = allowed & (key + (at - WINDOW) <= row)
            bias.append(jnp.where(allowed, 0.0, BELOW))
        bias = jnp.concatenate(bias, axis=0)
        span = pl.ds(first // ROWS, m * TILE // ROWS)

        def head(h, carry):
            at = lambda base: pl.ds(pl.multiple_of((base + h) * HEAD_DIM, HEAD_DIM), HEAD_DIM)
            q = q_ref[b, :, at(start)]
            k = held[span, :, at(0)].reshape(m * TILE, HEAD_DIM)
            v = held[span, :, at(heads)].reshape(m * TILE, HEAD_DIM)
            scores = bias + lax.dot_general(
                k, q, (((1,), (1,)), ((), ())), preferred_element_type=jnp.float32
            )
            row_max = jnp.max(scores, axis=0, keepdims=True)
            probs = jnp.exp2((scores - row_max) * scale)
            totals = jnp.sum(probs, axis=0, keepdims=True)
            mixed = lax.dot_general(
                v, probs.astype(jnp.bfloat16), (((0,), (0,)), ((), ())), preferred_element_type=jnp.float32
            )
            out_ref[b, :, at(0)] = (mixed / totals).T.astype(jnp.bfloat16)
            return carry

        if heads <= UNROLLED:
            for h in range(heads):
                head(h, 0)
        else:
            lax.fori_loop(0, heads, head, 0)

    def kernel(plan_ref, lows_ref, q_ref, local_ref, near_ref, far_ref, out_ref, held):
        held[...] = jnp.zeros_like(held)

        def stretch(b, carry):
            held[halo:] = local_ref[b, :, : 2 * wide].reshape(chunk, ROWS, 2 * wide)
            for ref, at, end in ((near_ref, 0, halo), (far_ref, 2, halo - chunk)):
                first, count = plan_ref[at, b], plan_ref[at + 1, b]

                def move(j, carry, ref=ref, first=first, to=end - count):
                    held[to + j] = ref[first + j]
                    return carry

                lax.fori_loop(0, count, move, 0)

            need = plan_ref[4, b]
            for less, m in zip((0, *spans), spans):
                pl.when((need > less) & (need <= m))(functools.partial(attend, m, b, lows_ref, q_ref, out_ref, held))
            return carry

        lax.fori_loop(0, stretches, stretch, 0)

    return pl.pallas_call(
        kernel,
        out_shape=jax.ShapeDtypeStruct((stretches, tokens, wide), query.dtype),
        in_specs=[pl.BlockSpec(memory_space=pltpu.SMEM)] + [pl.BlockSpec(memory_space=pltpu.VMEM)] * 5,
        out_specs=pl.BlockSpec(memory_space=pltpu.VMEM),
        scratch_shapes=[pltpu.VMEM((halo + chunk, ROWS, 2 * wide), jnp.bfloat16)],
        compiler_params=pltpu.CompilerParams(vmem_limit_bytes=32 * 1024 * 1024),
        cost_estimate=pl.CostEstimate(
            flops=4 * stretches * tokens * heads * HEAD_DIM * 3 * TILE,
            bytes_accessed=2 * (4 * stretches * tokens * wide + near.size + far.size),
            transcendentals=stretches * tokens * heads * 3 * TILE,
        ),
        name="attention",
    )(plan, lows, query, local, near, far)


def shards(groups, ring, queries, keys, values, doc_start):
    tokens = queries.shape[0]
    group_heads = max(1, 3 * HEADS // (4 * groups))
    rest_heads = HEADS - groups * group_heads
    chunk = tokens // ROWS
    chunks = groups * ring
    plane = lax.axis_index("uly")
    me = lax.axis_index("blk") * ring + plane

    def spread(array):
        return lax.all_to_all(array, "blk", split_axis=0, concat_axis=0, tiled=True)

    def onward(array):
        return lax.ppermute(array, "uly", [(i, (i + 1) % ring) for i in range(ring)])

    def next_chunk(array):
        return lax.ppermute(array, ("blk", "uly"), [(i, i + 1) for i in range(chunks - 1)])

    wide, rest = group_heads * HEAD_DIM, rest_heads * HEAD_DIM
    own_pair = rest_of(keys, values, rest)
    own_next = next_chunk(own_pair)
    own_after = next_chunk(own_next)

    lanes = lax.optimization_barrier((doc_start, own_pair))[0].reshape(1, -1, 128)
    starts = spread(jnp.broadcast_to(lanes, (groups, *lanes.shape[1:])))
    by_chunk = starts.reshape(chunks, tokens)
    opens = jnp.arange(chunks, dtype=jnp.int32) * tokens
    need = jnp.minimum(opens - by_chunk[:, 0], WINDOW - 1)
    near_need = (jnp.minimum(need, tokens) + ROWS - 1) // ROWS
    far_need = (jnp.maximum(need - tokens, 0) + ROWS - 1) // ROWS
    near_sum = jnp.max(jnp.sum(near_need.reshape(groups, ring), axis=0))
    far_sum = jnp.max(jnp.sum(far_need.reshape(groups, ring), axis=0))

    def mine(per_chunk, ahead):
        padded = jnp.concatenate([per_chunk, jnp.zeros((ring,), jnp.int32)])
        rolled = lax.dynamic_slice_in_dim(padded, plane + ahead, chunks, 0)
        return rolled.reshape(groups, ring)[:, 0]

    def before(counts):
        earlier = jnp.arange(groups)[None, :] < jnp.arange(groups)[:, None]
        return jnp.sum(jnp.where(earlier, counts[None, :], 0), axis=1)

    near_in, far_in = mine(near_need, 0), mine(far_need, 0)
    near_out, far_out = mine(near_need, 1), mine(far_need, 1)
    near_first = before(near_in)
    own_first = jnp.arange(groups, dtype=jnp.int32) * chunk + chunk - near_out
    near_plan = jnp.stack([own_first, before(near_out), near_out])
    far_plan = jnp.stack([near_first + near_in - far_out, before(far_out), far_out])

    position = jnp.arange(chunks * tokens, dtype=jnp.int32).reshape(chunks, tokens)
    lows = jnp.maximum(by_chunk, position - (WINDOW - 1)) - (opens[:, None] - WINDOW)
    tile_need = (WINDOW + tokens - lows[:, 0] + TILE - 1) // TILE
    lows = lows.astype(jnp.float32)
    plane_lows = lax.dynamic_index_in_dim(lows.reshape(groups, ring, tokens), plane, 1)
    plan = jnp.stack([near_first, near_in, before(far_in), far_in, mine(tile_need, 0)])

    def own(per_chunk):
        return lax.dynamic_index_in_dim(per_chunk, me, 0, keepdims=False)

    own_near, own_far = own(near_need), own(far_need)
    own_plan = jnp.stack([chunk - own_near, own_near, chunk - own_far, own_far, own(tile_need)])[:, None]
    own_lows = own(lows)[None, None]

    lead = (group_heads + 1) // 2
    tail = group_heads - lead
    pair, = split_heads((keys, values), groups, group_heads, (((0, 0, lead), (1, 0, lead)),))
    pair = spread(pair)
    most = (WINDOW + tokens) // TILE
    spans = (most - 3, most - 2, most)
    later = lax.optimization_barrier((keys, values, queries, starts))[:3]
    wanted = (((2, 0, lead),), ((2, 0, 0),)) + ((((0, lead, tail), (1, lead, tail), (2, lead, tail)),) if tail else ())
    query, own_query, *trio = split_heads(later, groups, group_heads, wanted)

    def run(room, pair, query, trio, near_plan, far_plan, plan, plane_lows, own_query, own_pair, own_next, own_after, own_plan, own_lows):
        near_slots, far_slots = (groups * chunk * share // 128 for share in room)
        as_blocks = lambda array: array.reshape(-1, ROWS, array.shape[2])
        tied = lambda array, *others: lax.optimization_barrier((array, others))[0]
        wide, narrow = 2 * lead * HEAD_DIM, 2 * tail * HEAD_DIM

        packed = pack(as_blocks(pair), near_plan, near_slots, wide)
        near = onward(packed)
        query = spread(tied(query, packed))
        if tail:
            (trio,) = (spread(tied(array, query)) for array in trio)
        passed = pack(near, far_plan, far_slots, wide, HINT)
        far = onward(passed)
        if tail:
            ready = pack(as_blocks(tied(trio, far)), near_plan, near_slots, narrow)
            near_tail = onward(ready)
            far = tied(far, ready)
        out = attention(plan, plane_lows, query, (0, lead), pair, near, far, spans)
        if tail:
            passed = pack(tied(near_tail, out), far_plan, far_slots, narrow, HINT)
            far_tail = onward(passed)
        done = [spread(out)]
        own_query = tied(own_query, passed, out)
        own_out = attention(
            own_plan, own_lows, own_query, (0, rest_heads), own_pair,
            as_blocks(own_next), as_blocks(own_after), spans[1:],
        )
        if tail:
            far_tail = tied(far_tail, own_out)
            out = attention(plan, plane_lows, trio, (2 * tail, tail), trio, near_tail, far_tail, spans)
            done.append(spread(tied(out, done)))
        return done, own_out

    shares = [[groups * chunk * share // 128 for share in room] for room in ROOMS]
    level = sum(
        ((near_sum > near) | (far_sum > far)).astype(jnp.int32) for near, far in shares[:-1]
    )
    done, own_out = lax.switch(
        level, [functools.partial(run, room) for room in ROOMS],
        pair, query, trio, near_plan, far_plan, plan, plane_lows, own_query, own_pair, own_next, own_after, own_plan, own_lows,
    )
    return join_heads(done, own_out)


def solution(mesh):
    return jax.shard_map(
        functools.partial(shards, mesh.shape["blk"], mesh.shape["uly"]),
        mesh=mesh,
        in_specs=(
            P(("blk", "uly"), None),
            P(("blk", "uly"), None),
            P(("blk", "uly"), None),
            P("blk"),
        ),
        out_specs=P(("blk", "uly"), None),
        check_vma=False,
    )
```

```python
import functools
import math

import jax
import jax.numpy as jnp
from jax import lax
from jax.experimental import pallas as pl
from jax.experimental.pallas import tpu as pltpu
from jax.sharding import PartitionSpec as P

HEADS = 32
HEAD_DIM = 128
WINDOW = 512
TILE = 128
ROWS = 16
BELOW = -1e30
HINT = 2 * 10**10
UNROLLED = 3
ROOMS = ((72, 25), (86, 36), (98, 49), (106, 71), (128, 128))


def split_heads(sources, groups, group_heads, wanted):
    tokens, columns = sources[0].shape
    band = group_heads * HEAD_DIM
    rest = columns - groups * band
    rows = min(64, tokens)
    shapes = [
        (groups if parts[0][2] else 1, rows, sum(size * HEAD_DIM or rest for _, _, size in parts))
        for parts in wanted
    ]

    def kernel(*refs):
        for out, parts in zip(refs[len(sources) :], wanted):
            to = 0
            for which, start, size in parts:
                wide = size * HEAD_DIM or rest
                for g in range(groups if size else 1):
                    first = g * band + start * HEAD_DIM if size else groups * band
                    out[g, :, to : to + wide] = refs[which][:, first : first + wide]
                to += wide

    return pl.pallas_call(
        kernel,
        grid=(tokens // rows,),
        out_shape=[
            jax.ShapeDtypeStruct((shape[0], tokens, shape[2]), sources[0].dtype) for shape in shapes
        ],
        in_specs=[pl.BlockSpec((rows, columns), lambda t: (t, 0))] * len(sources),
        out_specs=[pl.BlockSpec(shape, lambda t: (0, t, 0)) for shape in shapes],
        cost_estimate=pl.CostEstimate(
            flops=0, bytes_accessed=4 * len(sources) * sources[0].size, transcendentals=0
        ),
        name="split_heads",
    )(*sources)


def rest_of(keys, values, rest):
    tokens, columns = keys.shape
    rows = min(128, tokens)

    def kernel(k_ref, v_ref, out_ref):
        out_ref[0, :, :rest] = k_ref[...]
        out_ref[0, :, rest:] = v_ref[...]

    return pl.pallas_call(
        kernel,
        grid=(tokens // rows,),
        out_shape=jax.ShapeDtypeStruct((1, tokens, 2 * rest), keys.dtype),
        in_specs=[pl.BlockSpec((rows, rest), lambda t: (t, columns // rest - 1))] * 2,
        out_specs=pl.BlockSpec((1, rows, 2 * rest), lambda t: (0, t, 0)),
        cost_estimate=pl.CostEstimate(flops=0, bytes_accessed=8 * tokens * rest, transcendentals=0),
        name="rest_of",
    )(keys, values)


def join_heads(pieces, rest):
    groups, tokens, _ = pieces[0].shape
    band = sum(piece.shape[2] for piece in pieces)
    rows = min(128, tokens)

    def kernel(*refs):
        ins, other, out = refs[:-2], refs[-2], refs[-1]
        for g in range(groups):
            first = g * band
            for src in ins:
                out[:, first : first + src.shape[2]] = src[g]
                first += src.shape[2]
        out[:, groups * band :] = other[0]

    columns = groups * band + rest.shape[2]
    return pl.pallas_call(
        kernel,
        grid=(tokens // rows,),
        out_shape=jax.ShapeDtypeStruct((tokens, columns), rest.dtype),
        in_specs=[
            pl.BlockSpec((piece.shape[0], rows, piece.shape[2]), lambda t: (0, t, 0))
            for piece in (*pieces, rest)
        ],
        out_specs=pl.BlockSpec((rows, columns), lambda t: (t, 0)),
        cost_estimate=pl.CostEstimate(flops=0, bytes_accessed=4 * tokens * columns, transcendentals=0),
        name="join_heads",
    )(*pieces, rest)


def pack(blocks, plan, slots, wide, hint=0):
    rows = blocks.shape[1]
    stretches = plan.shape[1]

    def kernel(plan_ref, in_ref, out_ref):
        def stretch(b, carry):
            src, dst, count = plan_ref[0, b], plan_ref[1, b], plan_ref[2, b]

            def move(j, carry):
                out_ref[dst + j] = in_ref[src + j, :, :wide]
                return carry

            return lax.fori_loop(0, count, move, carry)

        lax.fori_loop(0, stretches, stretch, 0)

    return pl.pallas_call(
        kernel,
        out_shape=jax.ShapeDtypeStruct((slots, rows, wide), blocks.dtype),
        in_specs=[pl.BlockSpec(memory_space=pltpu.SMEM), pl.BlockSpec(memory_space=pltpu.VMEM)],
        out_specs=pl.BlockSpec(memory_space=pltpu.VMEM),
        compiler_params=pltpu.CompilerParams(vmem_limit_bytes=32 * 1024 * 1024),
        cost_estimate=pl.CostEstimate(
            flops=hint, bytes_accessed=4 * slots * rows * wide, transcendentals=0
        ),
        name="pack_halo",
    )(plan, blocks)


def attention(plan, lows, query, query_heads, local, near, far, spans):
    start, heads = query_heads
    stretches, tokens, _ = query.shape
    wide = heads * HEAD_DIM
    halo = WINDOW // ROWS
    chunk = tokens // ROWS
    scale = math.log2(math.e) / math.sqrt(HEAD_DIM)

    def attend(m, b, lows_ref, q_ref, out_ref, held):
        first = WINDOW + tokens - m * TILE
        key = lax.broadcasted_iota(jnp.int32, (TILE, tokens), 0)
        row = lax.broadcasted_iota(jnp.int32, (TILE, tokens), 1)
        low = jnp.broadcast_to(lows_ref[b], (TILE, tokens))
        bias = []
        for j in range(m):
            at = first + j * TILE
            allowed = (key + at).astype(jnp.float32) >= low
            if at + TILE > WINDOW:
                allowed = allowed & (key + (at - WINDOW) <= row)
            bias.append(jnp.where(allowed, 0.0, BELOW))
        bias = jnp.concatenate(bias, axis=0)
        span = pl.ds(first // ROWS, m * TILE // ROWS)

        def head(h, carry):
            at = lambda base: pl.ds(pl.multiple_of((base + h) * HEAD_DIM, HEAD_DIM), HEAD_DIM)
            q = q_ref[b, :, at(start)]
            k = held[span, :, at(0)].reshape(m * TILE, HEAD_DIM)
            v = held[span, :, at(heads)].reshape(m * TILE, HEAD_DIM)
            scores = bias + lax.dot_general(
                k, q, (((1,), (1,)), ((), ())), preferred_element_type=jnp.float32
            )
            row_max = jnp.max(scores, axis=0, keepdims=True)
            probs = jnp.exp2((scores - row_max) * scale)
            totals = jnp.sum(probs, axis=0, keepdims=True)
            mixed = lax.dot_general(
                v, probs.astype(jnp.bfloat16), (((0,), (0,)), ((), ())), preferred_element_type=jnp.float32
            )
            out_ref[b, :, at(0)] = (mixed / totals).T.astype(jnp.bfloat16)
            return carry

        if heads <= UNROLLED:
            for h in range(heads):
                head(h, 0)
        else:
            lax.fori_loop(0, heads, head, 0)

    def kernel(plan_ref, lows_ref, q_ref, local_ref, near_ref, far_ref, out_ref, held):
        held[...] = jnp.zeros_like(held)

        def stretch(b, carry):
            held[halo:] = local_ref[b, :, : 2 * wide].reshape(chunk, ROWS, 2 * wide)
            for ref, at, end in ((near_ref, 0, halo), (far_ref, 2, halo - chunk)):
                first, count = plan_ref[at, b], plan_ref[at + 1, b]

                def move(j, carry, ref=ref, first=first, to=end - count):
                    held[to + j] = ref[first + j]
                    return carry

                lax.fori_loop(0, count, move, 0)

            need = plan_ref[4, b]
            for less, m in zip((0, *spans), spans):
                pl.when((need > less) & (need <= m))(functools.partial(attend, m, b, lows_ref, q_ref, out_ref, held))
            return carry

        lax.fori_loop(0, stretches, stretch, 0)

    return pl.pallas_call(
        kernel,
        out_shape=jax.ShapeDtypeStruct((stretches, tokens, wide), query.dtype),
        in_specs=[pl.BlockSpec(memory_space=pltpu.SMEM)] + [pl.BlockSpec(memory_space=pltpu.VMEM)] * 5,
        out_specs=pl.BlockSpec(memory_space=pltpu.VMEM),
        scratch_shapes=[pltpu.VMEM((halo + chunk, ROWS, 2 * wide), jnp.bfloat16)],
        compiler_params=pltpu.CompilerParams(vmem_limit_bytes=32 * 1024 * 1024),
        cost_estimate=pl.CostEstimate(
            flops=4 * stretches * tokens * heads * HEAD_DIM * 3 * TILE,
            bytes_accessed=2 * (4 * stretches * tokens * wide + near.size + far.size),
            transcendentals=stretches * tokens * heads * 3 * TILE,
        ),
        name="attention",
    )(plan, lows, query, local, near, far)


def shards(groups, ring, queries, keys, values, doc_start):
    tokens = queries.shape[0]
    group_heads = max(1, 3 * HEADS // (4 * groups))
    rest_heads = HEADS - groups * group_heads
    chunk = tokens // ROWS
    chunks = groups * ring
    plane = lax.axis_index("uly")
    me = lax.axis_index("blk") * ring + plane

    def spread(array):
        return lax.all_to_all(array, "blk", split_axis=0, concat_axis=0, tiled=True)

    def onward(array):
        return lax.ppermute(array, "uly", [(i, (i + 1) % ring) for i in range(ring)])

    def next_chunk(array):
        return lax.ppermute(array, ("blk", "uly"), [(i, i + 1) for i in range(chunks - 1)])

    wide, rest = group_heads * HEAD_DIM, rest_heads * HEAD_DIM
    own_pair = rest_of(keys, values, rest)
    own_next = next_chunk(own_pair)
    own_after = next_chunk(own_next)

    lanes = lax.optimization_barrier((doc_start, own_pair))[0].reshape(1, -1, 128)
    starts = spread(jnp.broadcast_to(lanes, (groups, *lanes.shape[1:])))
    by_chunk = starts.reshape(chunks, tokens)
    opens = jnp.arange(chunks, dtype=jnp.int32) * tokens
    need = jnp.minimum(opens - by_chunk[:, 0], WINDOW - 1)
    near_need = (jnp.minimum(need, tokens) + ROWS - 1) // ROWS
    far_need = (jnp.maximum(need - tokens, 0) + ROWS - 1) // ROWS
    near_sum = jnp.max(jnp.sum(near_need.reshape(groups, ring), axis=0))
    far_sum = jnp.max(jnp.sum(far_need.reshape(groups, ring), axis=0))

    def mine(per_chunk, ahead):
        padded = jnp.concatenate([per_chunk, jnp.zeros((ring,), jnp.int32)])
        rolled = lax.dynamic_slice_in_dim(padded, plane + ahead, chunks, 0)
        return rolled.reshape(groups, ring)[:, 0]

    def before(counts):
        earlier = jnp.arange(groups)[None, :] < jnp.arange(groups)[:, None]
        return jnp.sum(jnp.where(earlier, counts[None, :], 0), axis=1)

    near_in, far_in = mine(near_need, 0), mine(far_need, 0)
    near_out, far_out = mine(near_need, 1), mine(far_need, 1)
    near_first = before(near_in)
    own_first = jnp.arange(groups, dtype=jnp.int32) * chunk + chunk - near_out
    near_plan = jnp.stack([own_first, before(near_out), near_out])
    far_plan = jnp.stack([near_first + near_in - far_out, before(far_out), far_out])

    position = jnp.arange(chunks * tokens, dtype=jnp.int32).reshape(chunks, tokens)
    lows = jnp.maximum(by_chunk, position - (WINDOW - 1)) - (opens[:, None] - WINDOW)
    tile_need = (WINDOW + tokens - lows[:, 0] + TILE - 1) // TILE
    lows = lows.astype(jnp.float32)
    plane_lows = lax.dynamic_index_in_dim(lows.reshape(groups, ring, tokens), plane, 1)
    plan = jnp.stack([near_first, near_in, before(far_in), far_in, mine(tile_need, 0)])

    def own(per_chunk):
        return lax.dynamic_index_in_dim(per_chunk, me, 0, keepdims=False)

    own_near, own_far = own(near_need), own(far_need)
    own_plan = jnp.stack([chunk - own_near, own_near, chunk - own_far, own_far, own(tile_need)])[:, None]
    own_lows = own(lows)[None, None]

    lead = (group_heads + 1) // 2
    tail = group_heads - lead
    pair, = split_heads((keys, values), groups, group_heads, (((0, 0, lead), (1, 0, lead)),))
    pair = spread(pair)
    most = (WINDOW + tokens) // TILE
    spans = (most - 3, most - 2, most)
    later = lax.optimization_barrier((keys, values, queries, starts))[:3]
    wanted = (((2, 0, lead),), ((2, 0, 0),)) + ((((0, lead, tail), (1, lead, tail), (2, lead, tail)),) if tail else ())
    query, own_query, *trio = split_heads(later, groups, group_heads, wanted)

    def run(room, pair, query, trio, near_plan, far_plan, plan, plane_lows, own_query, own_pair, own_next, own_after, own_plan, own_lows):
        near_slots, far_slots = (groups * chunk * share // 128 for share in room)
        as_blocks = lambda array: array.reshape(-1, ROWS, array.shape[2])
        tied = lambda array, *others: lax.optimization_barrier((array, others))[0]
        wide, narrow = 2 * lead * HEAD_DIM, 2 * tail * HEAD_DIM

        packed = pack(as_blocks(pair), near_plan, near_slots, wide)
        near = onward(packed)
        query = spread(tied(query, packed))
        if tail:
            (trio,) = (spread(tied(array, query)) for array in trio)
        passed = pack(near, far_plan, far_slots, wide, HINT)
        far = onward(passed)
        if tail:
            ready = pack(as_blocks(tied(trio, far)), near_plan, near_slots, narrow)
            near_tail = onward(ready)
            far = tied(far, ready)
        out = attention(plan, plane_lows, query, (0, lead), pair, near, far, spans)
        if tail:
            passed = pack(tied(near_tail, out), far_plan, far_slots, narrow, HINT)
            far_tail = onward(passed)
        done = [spread(out)]
        own_query = tied(own_query, passed, out)
        own_out = attention(
            own_plan, own_lows, own_query, (0, rest_heads), own_pair,
            as_blocks(own_next), as_blocks(own_after), spans[1:],
        )
        if tail:
            far_tail = tied(far_tail, own_out)
            out = attention(plan, plane_lows, trio, (2 * tail, tail), trio, near_tail, far_tail, spans)
            done.append(spread(tied(out, done)))
        return done, own_out

    shares = [[groups * chunk * share // 128 for share in room] for room in ROOMS]
    level = sum(
        ((near_sum > near) | (far_sum > far)).astype(jnp.int32) for near, far in shares[:-1]
    )
    done, own_out = lax.switch(
        level, [functools.partial(run, room) for room in ROOMS],
        pair, query, trio, near_plan, far_plan, plan, plane_lows, own_query, own_pair, own_next, own_after, own_plan, own_lows,
    )
    return join_heads(done, own_out)


def solution(mesh):
    return jax.shard_map(
        functools.partial(shards, mesh.shape["blk"], mesh.shape["uly"]),
        mesh=mesh,
        in_specs=(
            P(("blk", "uly"), None),
            P(("blk", "uly"), None),
            P(("blk", "uly"), None),
            P("blk"),
        ),
        out_specs=P(("blk", "uly"), None),
        check_vma=False,
    )
```
